256 devices in a mesh: src: 128 (over x, z, y), tgt: 2 (over core).
Axes of the slice: x: 4, y: 4, z: 8, core: 2. Of those that a mesh axis runs over, the one named last changes fastest.
Arguments:
- x_src: bfloat16 [64, 524288], P(None, 'src'), may hold values from -6 to 6
- w_src: float32 [524288], P('src'), may hold values from 13 to 310
- y_tgt: bfloat16 [64, 2097152], P(None, 'src'), may hold values from -6 to 6
- g_in: bfloat16 [2097152], P('src'), may hold values from 0 to 31
- support_owner: int32 [2, 2048, 8], P('tgt', 'src'), may hold values from 0 to 127, all different within a row; in each aligned block of 16 rows (0 to 15, 16 to 31, ..., all dimensions but the last counted through in order) at most 2 rows name the same one
- support_local: int32 [2, 2048, 8], P('tgt', 'src'), may hold values from 0 to 31
- live_count: int32 [2, 2048], P('tgt', 'src'), may hold values from 5 to 8
Outputs:
- f_new: float32 [524288], P('src')
- g_new: float32 [2097152], P('src')
The draws below stay inside these ranges and needn't reach their ends.
Inputs may be any that keep to these rules, and one draw needn't show every extreme that they name: `support_owner`: in each list half the 8 owners named by one row block are distinct, and the 16 row blocks of one device name one owner in at most 2 slots of that half.
All inputs are finite; a program needn't handle non-finite values.
Results may differ from the reference program's by a relative error of at most 0.0003.
Values may be sent and summed in bfloat16 or wider, within the bound.
A program may use at most 64 MiB of HBM per device.

```python
import math
import jax
import jax.numpy as jnp
import numpy as np
from jax import lax

DIM = 64
BLK = 256
KH = 8
RB_DEV = 16
TB_DEV = 64
MOST = 2
NRB = 2048
NTB = 8192
NS = 524288
NT = 2097152
N_SRC = 128
N_TGT = 2


def draw_w_src(key, part):
    values = jax.random.uniform(key, (NS,), jnp.float32, 13.0, 17.0)
    return values


def draw_g_in(key, part):
    values = jax.random.uniform(key, (NT,), jnp.float32, 0.0, 1.0)
    return values.astype(jnp.bfloat16)


def set_ends(entries, stream_key, smallest, largest):
    extent = entries.shape
    place = [jax.random.randint(jax.random.fold_in(stream_key, axis), (), 0, extent[axis]) for axis in range(len(extent))]
    entries = entries.at[tuple(place)].set(smallest)
    longest = extent.index(max(extent))
    place[longest] = (place[longest] + 1) % extent[longest]
    return entries.at[tuple(place)].set(largest)


def shard_levels(rng, extent, cuts, smallest, largest):
    def one(axis_at, blocks):
        draws = jax.random.uniform(jax.random.fold_in(jax.random.fold_in(rng, 6), axis_at), (blocks,), jnp.float32, smallest / len(cuts), largest / len(cuts))
        return jnp.repeat(jnp.exp(draws), extent[axis_at] // blocks).reshape((-1,) + (1,) * (len(extent) - axis_at - 1))

    level = one(*cuts[0])
    for cut in cuts[1:]:
        level = level * one(*cut)
    return level


def deal_out(key, own, number, rows, amount, top, limit, skew):
    ranking = jax.random.permutation(key, amount)
    crowded, ordinary = shares(amount, rows * top, limit, skew, True), shares(amount, rows * top, limit, skew, False)
    places = jnp.arange(amount)

    def named(lengths, turn):
        used = int((lengths > 0).sum())
        fixed = max(1, used // 4)
        passed = fixed + (places - fixed + turn * (used - fixed)) % max(1, amount - fixed)
        return jnp.zeros((amount,), jnp.int32).at[ranking[jnp.where(places < fixed, places, passed)]].set(jnp.asarray(lengths, jnp.int32))

    lengths = jnp.where(number % 4 == 0, named(crowded, number // 4), named(ordinary, number - number // 4 - 1))
    mixed = jax.random.permutation(jax.random.fold_in(own, 3), amount)
    source_of, sink = mixed[0:amount // 2 * 2:2], mixed[1:amount // 2 * 2:2]
    margin = jnp.minimum(lengths[source_of] - 1, limit - lengths[sink]) // 2
    margin = jnp.where((source_of == ranking[0]) | (sink == ranking[0]) | (lengths[sink] == 0), 0, jnp.maximum(margin, 0))
    passed = jax.random.randint(jax.random.fold_in(own, 4), (amount // 2,), 0, 1 << 20) % (margin + 1)
    lengths = lengths.at[source_of].add(-passed).at[sink].add(passed)
    members = jnp.searchsorted(jnp.cumsum(lengths), jnp.arange(rows * top), side="right").astype(jnp.int32)
    grid = members.reshape(top, rows).T
    grid = grid[jax.random.permutation(jax.random.fold_in(own, 1), rows)]
    turn = jax.random.randint(jax.random.fold_in(own, 2), (rows, 1), 0, top)
    return jnp.take_along_axis(grid, (jnp.arange(top)[None, :] + turn) % top, axis=1)


def shares(amount, total, reach, lean, full):
    weights = [(1 << 20) // math.isqrt(standing ** lean) + 1 for standing in range(1, amount + 1)]
    largest = reach if full else min(reach, max(-(-total // amount), total * weights[0] // sum(weights)))
    least = 1 if total - largest >= amount - 1 else 0
    given, spare = [largest] + [least] * (amount - 1), total - largest - least * (amount - 1)
    while spare > 0:
        movable = [i for i in range(1, amount) if given[i] < largest] or [i for i in range(1, amount) if given[i] < reach]
        whole, remaining = sum([weights[i] for i in movable]), spare
        for i in movable:
            addition = min(reach - given[i], max(1, remaining * weights[i] // whole), spare)
            given[i] = given[i] + addition
            spare = spare - addition
    return np.array(given)


def centred(stream_key, extent, spread, limit, split=(), kind=jnp.bfloat16):
    factor_of = shard_levels(stream_key, extent, split, -0.22, 0.18) if split else 1.0
    values = jax.random.normal(stream_key, extent, jnp.float32) * spread * factor_of
    return jnp.minimum(jnp.maximum(values, -limit), limit).astype(kind)


def setup_inputs(seed: int = 0) -> dict:
    key_of = jax.random.split(jax.random.key(seed), 8)
    x_src = centred(key_of[0], (DIM, NS), 1.0, 6.0, ((1, 128),))
    w_src = draw_w_src(jax.random.fold_in(key_of[7], 71), 0)
    y_tgt = centred(key_of[2], (DIM, NT), 1.0, 6.0, ((1, 128),))
    g_in = draw_g_in(jax.random.fold_in(key_of[7], 71), 0)
    support_owner_keys = jax.random.split(jax.random.fold_in(key_of[4], 1), N_TGT * NRB // RB_DEV)
    support_owner_turns = jax.random.permutation(jax.random.fold_in(key_of[4], 3), N_TGT * NRB // RB_DEV)
    support_owner = jax.vmap(lambda own, number: deal_out(jax.random.fold_in(key_of[4], 2), own, number, RB_DEV, N_SRC, KH, MOST, 2))(support_owner_keys, support_owner_turns).reshape((N_TGT, NRB, KH))
    support_local = set_ends(jax.random.randint(key_of[5], (N_TGT, NRB, KH), 0, TB_DEV // 2), jax.random.fold_in(key_of[5], 1), 0, (TB_DEV // 2) - 1).astype(jnp.int32)
    live_count = set_ends(jax.random.randint(key_of[6], (N_TGT, NRB), KH - 3, KH + 1), jax.random.fold_in(key_of[6], 1), KH - 3, KH).astype(jnp.int32)
    return {"x_src": x_src, "w_src": w_src, "y_tgt": y_tgt, "g_in": g_in, "support_owner": support_owner, "support_local": support_local, "live_count": live_count}


EPSILON = 0.1
EMPTY = -1.0e30


def potential(peak_value, mass_sum):
    ceiling = jnp.maximum(peak_value, 0.0)
    return -EPSILON * (ceiling + jnp.log(jnp.exp(-ceiling) + mass_sum * jnp.exp(peak_value - ceiling)))


def reference(x_src, w_src, y_tgt, g_in, support_owner, support_local, live_count):
    source_rows = x_src.astype(jnp.float32).reshape(DIM, NRB, BLK).transpose(1, 0, 2)
    target_rows = y_tgt.astype(jnp.float32).reshape(DIM, NTB, BLK).transpose(1, 0, 2)
    source_squares = jnp.sum(source_rows * source_rows, axis=1)
    target_squares = jnp.sum(target_rows * target_rows, axis=1)
    target_pots = g_in.astype(jnp.float32).reshape(NTB, BLK)
    weight_rows = w_src.reshape(NRB, BLK)
    offset = (jnp.arange(N_TGT, dtype=jnp.int32) * (TB_DEV // 2))[:, None, None]
    blocks = (support_owner * TB_DEV + offset + support_local).astype(jnp.int32)
    blocks = jnp.transpose(blocks, (1, 0, 2)).reshape(NRB, N_TGT * KH)
    alive_mask = lax.broadcasted_iota(jnp.int32, (N_TGT, NRB, KH), 2) < live_count[:, :, None]
    alive_mask = jnp.transpose(alive_mask, (1, 0, 2)).reshape(NRB, N_TGT * KH)

    def scan_step(state_pair, inputs):
        col_peak, col_total = state_pair
        row_tile, row_square, row_weights, block_ids, alive = inputs
        col_tiles = target_rows[block_ids]
        col_squares = target_squares[block_ids]
        col_pots = target_pots[block_ids]
        cross_terms = jnp.einsum("dc,lde->lce", row_tile, col_tiles)
        tile_cost = (row_square[None, :, None] + col_squares[:, None, :] - 2.0 * cross_terms) / DIM
        logits = jnp.where(alive[:, None, None], (col_pots[:, None, :] - tile_cost) / EPSILON, EMPTY)
        peak_value = jnp.maximum(jnp.max(logits, axis=(0, 2)), 0.0)
        mass_sum = jnp.exp(-peak_value) + jnp.sum(jnp.exp(logits - peak_value[None, :, None]), axis=(0, 2))
        source_new = -EPSILON * (peak_value + jnp.log(mass_sum))
        column_logits = jnp.where(alive[:, None, None], (source_new[None, :, None] - tile_cost) / EPSILON + row_weights[None, :, None], EMPTY)
        tile_peak = jnp.max(column_logits, axis=1)
        tile_sum = jnp.where(alive[:, None], jnp.sum(jnp.exp(column_logits - tile_peak[:, None, :]), axis=1), 0.0)
        old_peak = col_peak[block_ids]
        new_peak = jnp.maximum(old_peak, tile_peak)
        new_total = col_total[block_ids] * jnp.exp(old_peak - new_peak) + tile_sum * jnp.exp(tile_peak - new_peak)
        return (col_peak.at[block_ids].set(new_peak), col_total.at[block_ids].set(new_total)), source_new

    start = (jnp.full((NTB, BLK), EMPTY, jnp.float32), jnp.zeros((NTB, BLK), jnp.float32))
    (col_peak, col_total), source_new = lax.scan(scan_step, start, (source_rows, source_squares, weight_rows, blocks, alive_mask))
    f_new = source_new.reshape(NS)
    g_new = potential(col_peak, col_total).reshape(NT)
    return (f_new, g_new)
```

```python
import jax
import jax.numpy as jnp
import numpy as np
from jax import lax
from jax.experimental import pallas as pl
from jax.experimental.pallas import tpu as pltpu
from jax.sharding import Mesh, PartitionSpec as P

DIM = 64
BLK = 256
KH = 8
RB_DEV = 16
TB_DEV = 64
HALF = TB_DEV // 2

EPSILON = 0.1
EMPTY = -1e30
PER = 2.0 / (DIM * EPSILON)
PER2 = PER * float(np.log2(np.e))
OFFSET = DIM / 2.0
LN2 = float(np.log(2.0))
AUG = 16
UNROLL = 2


def split3(row):
    high = row.astype(jnp.bfloat16).astype(jnp.float32)
    middle = (row - high).astype(jnp.bfloat16).astype(jnp.float32)
    low = row - high - middle
    at = lax.broadcasted_iota(jnp.int32, (AUG, BLK), 0)
    rows = jnp.where(at == 0, high, jnp.where(at == 1, middle, jnp.where(at == 2, low, 0.0)))
    return rows.astype(jnp.bfloat16)


def three_ones():
    at = lax.broadcasted_iota(jnp.int32, (AUG, BLK), 0)
    return jnp.where(at < 3, 1.0, 0.0).astype(jnp.bfloat16)


def tile_logits(left, right):
    return lax.dot_general(
        left, right, (((0,), (0,)), ((), ())), preferred_element_type=jnp.float32
    )


def peak_and_mass(tile):
    peak = jnp.max(tile, axis=0, keepdims=True)
    mass = jnp.sum(jnp.exp2((tile - peak) * PER2), axis=0, keepdims=True)
    return peak, mass


def lane_block(index):
    return pl.ds(pl.multiple_of(index * BLK, BLK), BLK)


def x_tile(x_ref, block):
    return x_ref[block // KH, :, lane_block(block % KH)]


def y_tile(y_ref, block):
    return y_ref[block // HALF, :, lane_block(block % HALF)]


def row_kernel(items_ref, count_ref, x_ref, y_ref, bias_ref, out_ref, slots):
    slots[...] = jnp.full(slots.shape, EMPTY, jnp.float32)
    ones = three_ones()

    def step(group, carry):
        for k in range(UNROLL):
            code = items_ref[group * UNROLL + k]
            row, col = code // 256, code % 256
            safe = col % 128
            left = jnp.concatenate(
                [y_tile(y_ref, safe), split3(bias_ref[pl.ds(safe, 1), :])], axis=0
            )
            right = jnp.concatenate([x_tile(x_ref, row), ones], axis=0)
            peak, mass = peak_and_mass(tile_logits(left, right))
            slots[col // HALF, pl.ds(row, 1), :] = peak * PER2 + jnp.log2(mass)
        return carry

    lax.fori_loop(0, (count_ref[0] + UNROLL - 1) // UNROLL, step, 0)
    parts = [slots[k] for k in range(4)]
    top = jnp.maximum(jnp.maximum(parts[0], parts[1]), jnp.maximum(parts[2], parts[3]))
    total = sum(jnp.exp2(part - top) for part in parts)
    out_ref[...] = top + jnp.log2(total)


def column_kernel(items_ref, count_ref, x_ref, y_ref, bias_ref, out_ref, peaks, masses):
    peaks[...] = jnp.full(peaks.shape, EMPTY, jnp.float32)
    masses[...] = jnp.zeros(masses.shape, jnp.float32)
    ones = three_ones()

    def step(group, carry):
        for k in range(UNROLL):
            code = items_ref[group * UNROLL + k]
            row, col = code // 256, code % 256
            left = jnp.concatenate(
                [x_tile(x_ref, row), split3(bias_ref[pl.ds(row, 1), :])], axis=0
            )
            right = jnp.concatenate([y_tile(y_ref, col % 128), ones], axis=0)
            peak, mass = peak_and_mass(tile_logits(left, right))
            old = peaks[pl.ds(col, 1), :]
            new = jnp.maximum(old, peak)
            peaks[pl.ds(col, 1), :] = new
            masses[pl.ds(col, 1), :] = masses[pl.ds(col, 1), :] * jnp.exp2(
                (old - new) * PER2
            ) + mass * jnp.exp2((peak - new) * PER2)
        return carry

    lax.fori_loop(0, (count_ref[0] + UNROLL - 1) // UNROLL, step, 0)
    mass = masses[0:128, :]
    out_ref[...] = jnp.where(mass > 0.0, peaks[0:128, :] * PER2 + jnp.log2(mass), EMPTY)


SMEM = pl.BlockSpec(memory_space=pltpu.SMEM)
VMEM = pl.BlockSpec(memory_space=pltpu.VMEM)


def local_call(body, out_rows, scratch, name):
    return pl.pallas_call(
        body,
        out_shape=jax.ShapeDtypeStruct((out_rows, BLK), jnp.float32),
        in_specs=[SMEM, SMEM, VMEM, VMEM, VMEM],
        out_specs=VMEM,
        scratch_shapes=scratch,
        compiler_params=pltpu.CompilerParams(vmem_limit_bytes=48 * 1024 * 1024),
        name=name,
    )


def half_squares(tile):
    return 0.5 * jnp.sum(jnp.square(tile.astype(jnp.float32)), axis=0)


def potential(logit2):
    logit = logit2 * LN2
    top = jnp.maximum(logit, 0.0)
    return -EPSILON * (top + jnp.log(jnp.exp(-top) + jnp.exp(logit - top)))


def merged(parts):
    top = jnp.max(parts, axis=0)
    return top + jnp.log2(jnp.sum(jnp.exp2(parts - top[None]), axis=0))


def on_device(x_src, w_src, y_tgt, g_in, support_owner, support_local, live_count):
    core = lax.axis_index("core")
    here = lax.axis_index("z") * lax.axis_size("y") + lax.axis_index("y")
    plane = ("z", "y", "core")
    lines = lax.axis_size("z") * lax.axis_size("y")
    rows = lines * RB_DEV
    half_rows = RB_DEV // 2

    x_half = lax.dynamic_slice_in_dim(x_src, core * half_rows * BLK, half_rows * BLK, 1)
    w_half = lax.dynamic_slice_in_dim(w_src, core * half_rows * BLK, half_rows * BLK, 0)
    y_half = lax.dynamic_slice_in_dim(y_tgt, core * HALF * BLK, HALF * BLK, 1)
    g_half = lax.dynamic_slice_in_dim(g_in, core * HALF * BLK, HALF * BLK, 0)
    x_squares = half_squares(x_half)
    y_squares = half_squares(y_half)
    y_bias = OFFSET * g_half.astype(jnp.float32) - y_squares

    live = lax.broadcasted_iota(jnp.int32, (RB_DEV, KH), 1) < live_count[0][:, None]
    listed = jnp.where(live, support_owner[0] * HALF + support_local[0], -1)
    listed = lax.all_gather(listed.T, ("z", "y"), axis=1, tiled=True)
    x_all = lax.all_gather(x_half, plane)
    y_all = lax.all_gather(y_half, "x")
    bias_all = lax.all_gather(y_bias.reshape(HALF, BLK), "x", tiled=True)

    owner = listed // HALF
    match = (listed >= 0) & (owner % lines == here)
    codes = (
        lax.broadcasted_iota(jnp.int32, (KH, rows), 1) * 256
        + (owner // lines) * HALF
        + listed % HALF
    )
    hits = match.astype(jnp.int32)
    per_row = jnp.sum(hits, axis=0)
    order = lax.iota(jnp.int32, rows)
    before = jnp.sum(jnp.where(order[:, None] < order[None, :], per_row[:, None], 0), axis=0)
    earlier = jnp.concatenate(
        [jnp.sum(hits[:k], axis=0, keepdims=True) for k in range(KH)], axis=0
    )
    place = jnp.where(match, before[None, :] + earlier, -1)
    most = 256
    spot = lax.iota(jnp.int32, most)
    items = jnp.sum(
        jnp.where(spot[:, None, None] == place[None], codes[None], 0), axis=(1, 2)
    )
    count = jnp.sum(per_row)
    items = jnp.where(spot < count, items, 128)
    count = count.reshape(1)

    partial = local_call(
        row_kernel, rows, [pltpu.VMEM((5, rows, BLK), jnp.float32)], "rows"
    )(items, count, x_all, y_all, bias_all)
    partial = lax.all_to_all(
        partial.reshape(2 * lines, half_rows, BLK), plane, split_axis=0, concat_axis=0, tiled=True
    )
    squares = x_squares.reshape(half_rows, BLK)
    f_half = potential(merged(partial) - PER2 * squares)
    col_bias = (
        OFFSET * f_half
        + (EPSILON * OFFSET) * w_half.reshape(half_rows, BLK)
        - squares
    )
    bias_rows = lax.all_gather(col_bias, plane, tiled=True)
    f_new = lax.all_gather(f_half, "core", tiled=True)

    col = local_call(
        column_kernel,
        4 * HALF,
        [pltpu.VMEM((136, BLK), jnp.float32), pltpu.VMEM((136, BLK), jnp.float32)],
        "columns",
    )(items, count, x_all, y_all, bias_rows)
    col = lax.all_to_all(
        col.reshape(4, HALF, BLK), "x", split_axis=0, concat_axis=0, tiled=True
    )
    g_half = potential(merged(col) - PER2 * y_squares.reshape(HALF, BLK))
    g_new = lax.all_gather(g_half, "core", tiled=True)
    return f_new.reshape(RB_DEV * BLK), g_new.reshape(TB_DEV * BLK)


def solution(mesh):
    fine = Mesh(mesh.devices.reshape(4, 8, 4, 2), ("x", "z", "y", "core"))
    src = ("x", "z", "y")
    placed = (
        P(None, src),
        P(src),
        P(None, src),
        P(src),
        P("core", src, None),
        P("core", src, None),
        P("core", src),
    )
    return jax.shard_map(
        on_device, mesh=fine, in_specs=placed, out_specs=(P(src), P(src)), check_vma=False
    )
```

```python
import functools
import heapq

import jax
import jax.numpy as jnp
import numpy as np
from jax import lax
from jax.experimental import pallas as pl
from jax.experimental.pallas import tpu as pltpu
from jax.sharding import Mesh, PartitionSpec as P

DIM = 64
BLK = 256
KH = 8
RB_DEV = 16
TB_DEV = 64
HALF = TB_DEV // 2

EPSILON = 0.1
EMPTY = -1e30
PER = 2.0 / (DIM * EPSILON)
PER2 = PER * float(np.log2(np.e))
OFFSET = DIM / 2.0
LN2 = float(np.log(2.0))
AUG = 16
UNROLL = 2


def split3(row):
    high = row.astype(jnp.bfloat16).astype(jnp.float32)
    middle = (row - high).astype(jnp.bfloat16).astype(jnp.float32)
    low = row - high - middle
    at = lax.broadcasted_iota(jnp.int32, (AUG, BLK), 0)
    rows = jnp.where(at == 0, high, jnp.where(at == 1, middle, jnp.where(at == 2, low, 0.0)))
    return rows.astype(jnp.bfloat16)


def three_ones():
    at = lax.broadcasted_iota(jnp.int32, (AUG, BLK), 0)
    return jnp.where(at < 3, 1.0, 0.0).astype(jnp.bfloat16)


def tile_logits(left, right):
    return lax.dot_general(
        left, right, (((0,), (0,)), ((), ())), preferred_element_type=jnp.float32
    )


def peak_and_mass(tile):
    peak = jnp.max(tile, axis=0, keepdims=True)
    mass = jnp.sum(jnp.exp2((tile - peak) * PER2), axis=0, keepdims=True)
    return peak, mass


def lane_block(index):
    return pl.ds(pl.multiple_of(index * BLK, BLK), BLK)


def x_tile(x_ref, block):
    return x_ref[block // KH, :, lane_block(block % KH)]


def y_tile(y_ref, block):
    return y_ref[block // HALF, :, lane_block(block % HALF)]


def row_kernel(items_ref, x_ref, y_ref, bias_ref, out_ref, slots):
    slots[...] = jnp.full(slots.shape, EMPTY, jnp.float32)
    ones = three_ones()

    def step(group, carry):
        for k in range(UNROLL):
            code = items_ref[0, group * UNROLL + k]
            row, col = code // 256, code % 256
            safe = col % 128
            left = jnp.concatenate(
                [y_tile(y_ref, safe), split3(bias_ref[pl.ds(safe, 1), :])], axis=0
            )
            right = jnp.concatenate([x_tile(x_ref, row), ones], axis=0)
            peak, mass = peak_and_mass(tile_logits(left, right))
            slots[col // HALF, pl.ds(row, 1), :] = peak * PER2 + jnp.log2(mass)
        return carry

    lax.fori_loop(0, (items_ref[1, 0] + UNROLL - 1) // UNROLL, step, 0)
    parts = [slots[k] for k in range(4)]
    top = jnp.maximum(jnp.maximum(parts[0], parts[1]), jnp.maximum(parts[2], parts[3]))
    total = sum(jnp.exp2(part - top) for part in parts)
    out_ref[...] = top + jnp.log2(total)


def column_kernel(items_ref, x_ref, y_ref, bias_ref, out_ref, peaks, masses):
    peaks[...] = jnp.full(peaks.shape, EMPTY, jnp.float32)
    masses[...] = jnp.zeros(masses.shape, jnp.float32)
    ones = three_ones()

    def step(group, carry):
        for k in range(UNROLL):
            code = items_ref[0, group * UNROLL + k]
            row, col = code // 256, code % 256
            left = jnp.concatenate(
                [x_tile(x_ref, row), split3(bias_ref[pl.ds(row, 1), :])], axis=0
            )
            right = jnp.concatenate([y_tile(y_ref, col % 128), ones], axis=0)
            peak, mass = peak_and_mass(tile_logits(left, right))
            old = peaks[pl.ds(col, 1), :]
            new = jnp.maximum(old, peak)
            peaks[pl.ds(col, 1), :] = new
            masses[pl.ds(col, 1), :] = masses[pl.ds(col, 1), :] * jnp.exp2(
                (old - new) * PER2
            ) + mass * jnp.exp2((peak - new) * PER2)
        return carry

    lax.fori_loop(0, (items_ref[1, 0] + UNROLL - 1) // UNROLL, step, 0)
    mass = masses[0:128, :]
    out_ref[...] = jnp.where(mass > 0.0, peaks[0:128, :] * PER2 + jnp.log2(mass), EMPTY)


SMEM = pl.BlockSpec(memory_space=pltpu.SMEM)
VMEM = pl.BlockSpec(memory_space=pltpu.VMEM)


def local_call(body, out_rows, scratch, name):
    return pl.pallas_call(
        body,
        out_shape=jax.ShapeDtypeStruct((out_rows, BLK), jnp.float32),
        in_specs=[SMEM, VMEM, VMEM, VMEM],
        out_specs=VMEM,
        scratch_shapes=scratch,
        compiler_params=pltpu.CompilerParams(vmem_limit_bytes=48 * 1024 * 1024),
        name=name,
    )


MESH = pl.DeviceIdType.MESH
NX, NZ, NY, NC = 4, 8, 4, 2
LINES = NZ * NY
ROWS = LINES * RB_DEV
HALF_RB = RB_DEV // 2
MOST = LINES * KH
X_LANES = HALF_RB * BLK
Y_LANES = HALF * BLK
A_LANES = 3 * BLK
B_LANES = X_LANES - A_LANES
Y_CHUNKS = 4
CHUNK = Y_LANES // Y_CHUNKS


def anywhere():
    return pl.BlockSpec(memory_space=pl.ANY)


def place():
    return tuple(lax.axis_index(axis) for axis in ("x", "z", "y", "core"))


def moved(size, offset):
    longest = {8: 4, 4: 2}[size]
    shortest = size - 1 - longest
    out = []
    if -longest < offset <= 0:
        out.append((1, offset - 1))
    if 0 <= offset < shortest:
        out.append((-1, offset + 1))
    return out


def onward(piece):
    kind, a, b = piece
    if kind == "A":
        found = [("z", d, ("A", n, b)) for d, n in moved(NZ, a)]
        if a == 0:
            found += [("y", d, ("A", 0, n)) for d, n in moved(NY, b)]
    elif kind == "B":
        found = [("z", d, ("B", n, 0)) for d, n in moved(NZ, a)] if b == 0 else []
        found += [("y", d, ("B", a, n)) for d, n in moved(NY, b)]
    else:
        found = [("x", d, (kind, n, 0)) for d, n in moved(NX, a)]
    return found


def gather_plan():
    took = {"A": 2.0, "B": 2.0 * B_LANES / A_LANES, "Y": 2.0 * CHUNK / A_LANES}
    kinds = [f"Y{k}" for k in range(Y_CHUNKS)]
    first = [("B", 0, 0), ("A", 0, 0)] + [(k, 0, 0) for k in kinds]
    free, waiting, order = {}, [], []

    def send(now, piece):
        for axis, direction, seen in onward(piece):
            begin = max(now, free.get((axis, direction), 0.0))
            end = begin + took[piece[0][0]]
            free[axis, direction] = end
            heapq.heappush(waiting, (end + 1.0, seen))

    for piece in first:
        send(0.0, piece)
    while waiting:
        now, piece = heapq.heappop(waiting)
        order.append(piece)
        send(now, piece)
    return first, order


def gather_kernel(
    x_ref, y_ref, g_ref, list_ref,
    x_all, y_all, bias_all, squares_ref, items_ref,
    codes, x_own, y_own, bias_sem, code_sem, own_sem, keep_sem, x_send, y_send, pair_send, pair_recv, got,
):
    x, z, y, c = place()
    turn = 1 - 2 * c
    line = z * NY + y
    first, order = gather_plan()
    index = {piece: k for k, piece in enumerate(order)}

    barrier = pltpu.get_barrier_semaphore()

    def plane_peer(k):
        other = lax.rem(line + k, LINES)
        return (x, other // NY, other % NY, c)

    def greet(k, carry):
        pl.semaphore_signal(barrier, inc=1, device_id=plane_peer(k), device_id_type=MESH)
        return carry

    lax.fori_loop(1, LINES, greet, 0)
    for k in range(1, NX):
        pl.semaphore_signal(
            barrier, inc=1, device_id=(lax.rem(x + k, NX), z, y, c), device_id_type=MESH
        )
    sibling = (x, z, y, 1 - c)
    pl.semaphore_signal(barrier, inc=1, device_id=sibling, device_id_type=MESH)

    x_mine = pl.multiple_of(c * X_LANES, X_LANES)
    y_mine = pl.multiple_of(c * Y_LANES, Y_LANES)
    keeps = [
        pltpu.make_async_copy(
            x_ref.at[:, pl.ds(k * X_LANES, X_LANES)], x_all.at[line * 2 + k], keep_sem.at[k]
        )
        for k in range(2)
    ]
    keeps.append(
        pltpu.make_async_copy(y_ref.at[:, pl.ds(y_mine, Y_LANES)], y_all.at[x], keep_sem.at[2])
    )
    owns = [
        pltpu.make_async_copy(x_ref.at[:, pl.ds(x_mine, X_LANES)], x_own, own_sem.at[0]),
        pltpu.make_async_copy(y_ref.at[:, pl.ds(y_mine, Y_LANES)], y_own, own_sem.at[1]),
    ]
    for copy in owns + keeps:
        copy.start()
    pl.semaphore_wait(barrier, LINES - 1 + NX - 1 + 1)

    def lanes_of(kind):
        if kind == "A":
            return 0, A_LANES
        if kind == "B":
            return A_LANES, B_LANES
        return int(kind[1:]) * CHUNK, CHUNK

    def slot(piece):
        kind, a, b = piece
        begin, width = lanes_of(kind)
        if kind[0] == "Y":
            return y_all.at[lax.rem(x + turn * a + NX, NX), :, pl.ds(begin, width)]
        origin = lax.rem(z + turn * a + NZ, NZ) * NY + lax.rem(y + turn * b + NY, NY)
        return x_all.at[origin * 2 + c, :, pl.ds(begin, width)]

    def source(piece):
        kind, a, b = piece
        if a or b:
            return slot(piece)
        begin, width = lanes_of(kind)
        if kind[0] == "Y":
            return y_ref.at[:, pl.ds(pl.multiple_of(y_mine + begin, BLK), width)]
        return x_ref.at[:, pl.ds(pl.multiple_of(x_mine + begin, BLK), width)]

    def neighbour(axis, direction):
        step = turn * direction
        return (
            lax.rem(x + step + NX, NX) if axis == "x" else x,
            lax.rem(z + step + NZ, NZ) if axis == "z" else z,
            lax.rem(y + step + NY, NY) if axis == "y" else y,
            c,
        )

    def pass_on(piece):
        for axis, direction, seen in onward(piece):
            pltpu.make_async_remote_copy(
                src_ref=source(piece),
                dst_ref=slot(piece),
                send_sem=y_send if piece[0][0] == "Y" else x_send,
                recv_sem=got.at[index[seen]],
                device_id=neighbour(axis, direction),
                device_id_type=MESH,
            ).start()

    for piece in first:
        pass_on(piece)

    def send_codes(k, carry):
        pltpu.make_async_remote_copy(
            src_ref=list_ref,
            dst_ref=codes.at[line],
            send_sem=code_sem.at[0],
            recv_sem=code_sem.at[1],
            device_id=plane_peer(k),
            device_id_type=MESH,
        ).start()
        return carry

    lax.fori_loop(1, LINES, send_codes, 0)

    for copy in owns:
        copy.wait()

    def squares_of(tile):
        return 0.5 * jnp.sum(jnp.square(tile.astype(jnp.float32)), axis=0, keepdims=True)

    for k in range(HALF_RB):
        squares_ref[k : k + 1, :] = squares_of(x_own[:, k * BLK : (k + 1) * BLK])
    y_squares = [squares_of(y_own[:, k * BLK : (k + 1) * BLK]) for k in range(HALF)]
    for k in range(HALF):
        squares_ref[HALF_RB + k : HALF_RB + k + 1, :] = y_squares[k]
    own_bias = OFFSET * g_ref[...].astype(jnp.float32) - squares_ref[HALF_RB : HALF_RB + HALF, :]
    bias_all[x] = own_bias
    for k in range(1, NX):
        pltpu.make_async_remote_copy(
            src_ref=bias_all.at[x],
            dst_ref=bias_all.at[x],
            send_sem=bias_sem.at[0],
            recv_sem=bias_sem.at[1],
            device_id=(lax.rem(x + k, NX), z, y, c),
            device_id_type=MESH,
        ).start()

    def advance(pieces):
        for piece in pieces:
            here = slot(piece)
            pltpu.make_async_copy(here, here, got.at[index[piece]]).wait()
            pass_on(piece)
            if piece[0][0] != "Y":
                pltpu.make_async_remote_copy(
                    src_ref=here,
                    dst_ref=here,
                    send_sem=pair_send,
                    recv_sem=pair_recv,
                    device_id=sibling,
                    device_id_type=MESH,
                ).start()

    third = len(order) // 3
    advance(order[:third])

    codes[line] = list_ref[...]
    for side in range(2):
        pltpu.make_async_copy(
            codes.at[pl.ds(0, LINES - 1)], codes.at[pl.ds(0, LINES - 1)], code_sem.at[side]
        ).wait()
    table = codes[...].reshape(LINES, RB_DEV * KH)
    owner = table // HALF
    match = (table >= 0) & (owner % LINES == line)
    lane = lax.broadcasted_iota(jnp.int32, table.shape, 1)
    row = lax.broadcasted_iota(jnp.int32, table.shape, 0) * RB_DEV + lane // KH
    code = (row * 256 + (owner // LINES) * HALF + table % HALF).astype(jnp.float32)
    hits = match.astype(jnp.float32)
    wide = RB_DEV * KH
    over, down = (lax.broadcasted_iota(jnp.int32, (wide, wide), k) for k in range(2))
    exact = functools.partial(
        jnp.dot, preferred_element_type=jnp.float32, precision=lax.Precision.HIGHEST
    )
    left = exact(hits, (over < down).astype(jnp.float32))
    totals = exact(hits, jnp.ones((wide, wide), jnp.float32))
    over, down = (lax.broadcasted_iota(jnp.int32, (LINES, LINES), k) for k in range(2))
    above = exact((down < over).astype(jnp.float32), totals)
    count = jnp.sum(totals, axis=0, keepdims=True)
    spot_of = jnp.where(match, left + above, -1.0)
    spots = lax.broadcasted_iota(jnp.int32, (MOST, wide), 0).astype(jnp.float32)
    found = jnp.zeros((MOST, wide), jnp.float32)
    for k in range(LINES):
        found += jnp.where(spot_of[k : k + 1, :] == spots, code[k : k + 1, :], 0.0)
    items = lax.dot_general(
        jnp.ones((8, wide), jnp.float32),
        found,
        (((1,), (1,)), ((), ())),
        preferred_element_type=jnp.float32,
        precision=lax.Precision.HIGHEST,
    )
    many = jnp.concatenate([count] * (MOST // wide), axis=1)
    spot = lax.broadcasted_iota(jnp.int32, (8, MOST), 1).astype(jnp.float32)
    items = jnp.where(spot < many, items, 128.0)
    at = lax.broadcasted_iota(jnp.int32, (8, MOST), 0)
    items_ref[...] = jnp.where(at == 0, items, many).astype(jnp.int32)

    advance(order[third:])
    for copy in keeps:
        copy.wait()
    most_x = x_all.at[pl.ds(0, LINES - 1)]
    for semaphore in (x_send, pair_send, pair_recv):
        pltpu.make_async_copy(most_x, most_x, semaphore).wait()
    most_y = y_all.at[pl.ds(0, NX - 1)]
    pltpu.make_async_copy(most_y, most_y, y_send).wait()
    most_bias = bias_all.at[pl.ds(0, NX - 1)]
    for side in range(2):
        pltpu.make_async_copy(most_bias, most_bias, bias_sem.at[side]).wait()


def gather(x_src, y_tgt, g_half, listed):
    count = len(gather_plan()[1])
    dma = pltpu.SemaphoreType.DMA
    return pl.pallas_call(
        gather_kernel,
        out_shape=(
            jax.ShapeDtypeStruct((2 * LINES, DIM, X_LANES), jnp.bfloat16),
            jax.ShapeDtypeStruct((NX, DIM, Y_LANES), jnp.bfloat16),
            jax.ShapeDtypeStruct((NX, HALF, BLK), jnp.float32),
            jax.ShapeDtypeStruct((HALF_RB + HALF, BLK), jnp.float32),
            jax.ShapeDtypeStruct((8, MOST), jnp.int32),
        ),
        in_specs=[anywhere(), anywhere(), VMEM, VMEM],
        out_specs=(anywhere(), anywhere(), VMEM, VMEM, VMEM),
        scratch_shapes=[
            pltpu.VMEM((LINES, 1, RB_DEV * KH), jnp.int32),
            pltpu.VMEM((DIM, X_LANES), jnp.bfloat16),
            pltpu.VMEM((DIM, Y_LANES), jnp.bfloat16),
            dma((2,)),
            dma((2,)),
            dma((2,)),
            dma((3,)),
            dma,
            dma,
            dma,
            dma,
            dma((count,)),
        ],
        compiler_params=pltpu.CompilerParams(
            collective_id=0, has_side_effects=True, vmem_limit_bytes=24 * 1024 * 1024
        ),
        name="gather",
    )(x_src, y_tgt, g_half, listed)


def potential(logit2):
    logit = logit2 * LN2
    top = jnp.maximum(logit, 0.0)
    return -EPSILON * (top + jnp.log(jnp.exp(-top) + jnp.exp(logit - top)))


def merged(parts):
    top = functools.reduce(jnp.maximum, parts)
    return top + jnp.log2(sum(jnp.exp2(part - top) for part in parts))


def exchange_kernel(
    part_ref, w_ref, squares_ref, f_ref, bias_ref, parts, part_sem, bias_sem, f_sem
):
    x, z, y, c = place()
    group = NC * LINES
    me = (z * NY + y) * NC + c

    def peer(k):
        other = lax.rem(me + k, group)
        return other, (x, other // (NY * NC), (other // NC) % NY, other % NC)

    barrier = pltpu.get_barrier_semaphore()

    def greet(k, carry):
        pl.semaphore_signal(barrier, inc=1, device_id=peer(k)[1], device_id_type=MESH)
        return carry

    lax.fori_loop(1, group, greet, 0)
    pl.semaphore_wait(barrier, group - 1)

    def send_part(k, carry):
        other, device = peer(k)
        pltpu.make_async_remote_copy(
            src_ref=part_ref.at[other],
            dst_ref=parts.at[me],
            send_sem=part_sem.at[0],
            recv_sem=part_sem.at[1],
            device_id=device,
            device_id_type=MESH,
        ).start()
        return carry

    lax.fori_loop(1, group, send_part, 0)
    parts[me] = part_ref[me]
    others = parts.at[pl.ds(0, group - 1)]
    pltpu.make_async_copy(others, others, part_sem.at[1]).wait()
    squares = squares_ref[...]
    f_half = potential(merged([parts[k] for k in range(group)]) - PER2 * squares)
    mine = pl.ds(pl.multiple_of(c * HALF_RB, HALF_RB), HALF_RB)
    f_ref[mine, :] = f_half
    bias_ref[me] = OFFSET * f_half + (EPSILON * OFFSET) * w_ref[mine, :] - squares

    def send_bias(k, carry):
        pltpu.make_async_remote_copy(
            src_ref=bias_ref.at[me],
            dst_ref=bias_ref.at[me],
            send_sem=bias_sem.at[0],
            recv_sem=bias_sem.at[1],
            device_id=peer(k)[1],
            device_id_type=MESH,
        ).start()
        return carry

    lax.fori_loop(1, group, send_bias, 0)
    over = pltpu.make_async_remote_copy(
        src_ref=f_ref.at[mine, :],
        dst_ref=f_ref.at[mine, :],
        send_sem=f_sem.at[0],
        recv_sem=f_sem.at[1],
        device_id=(x, z, y, 1 - c),
        device_id_type=MESH,
    )
    over.start()
    pltpu.make_async_copy(others, others, part_sem.at[0]).wait()
    others = bias_ref.at[pl.ds(0, group - 1)]
    for side in range(2):
        pltpu.make_async_copy(others, others, bias_sem.at[side]).wait()
    over.wait()


def exchange(partial, w_rows, squares):
    dma = pltpu.SemaphoreType.DMA
    group = NC * LINES
    return pl.pallas_call(
        exchange_kernel,
        out_shape=(
            jax.ShapeDtypeStruct((RB_DEV, BLK), jnp.float32),
            jax.ShapeDtypeStruct((group, HALF_RB, BLK), jnp.float32),
        ),
        in_specs=[VMEM, VMEM, VMEM],
        out_specs=(VMEM, VMEM),
        scratch_shapes=[
            pltpu.VMEM((group, HALF_RB, BLK), jnp.float32),
            dma((2,)),
            dma((2,)),
            dma((2,)),
        ],
        compiler_params=pltpu.CompilerParams(
            collective_id=1, has_side_effects=True, vmem_limit_bytes=16 * 1024 * 1024
        ),
        name="exchange",
    )(partial, w_rows, squares)


def finish_kernel(part_ref, squares_ref, g_ref, parts, part_sem, g_sem):
    x, z, y, c = place()
    barrier = pltpu.get_barrier_semaphore()
    peers = [(lax.rem(x + k, NX), z, y, c) for k in range(1, NX)]
    sibling = (x, z, y, 1 - c)
    for device in peers + [sibling]:
        pl.semaphore_signal(barrier, inc=1, device_id=device, device_id_type=MESH)
    pl.semaphore_wait(barrier, NX)
    for device in peers:
        pltpu.make_async_remote_copy(
            src_ref=part_ref.at[device[0]],
            dst_ref=parts.at[x],
            send_sem=part_sem.at[0],
            recv_sem=part_sem.at[1],
            device_id=device,
            device_id_type=MESH,
        ).start()
    parts[x] = part_ref[x]
    others = parts.at[pl.ds(0, NX - 1)]
    pltpu.make_async_copy(others, others, part_sem.at[1]).wait()
    g_half = potential(merged([parts[k] for k in range(NX)]) - PER2 * squares_ref[...])
    mine = pl.ds(pl.multiple_of(c * HALF, HALF), HALF)
    g_ref[mine, :] = g_half
    over = pltpu.make_async_remote_copy(
        src_ref=g_ref.at[mine, :],
        dst_ref=g_ref.at[mine, :],
        send_sem=g_sem.at[0],
        recv_sem=g_sem.at[1],
        device_id=sibling,
        device_id_type=MESH,
    )
    over.start()
    pltpu.make_async_copy(others, others, part_sem.at[0]).wait()
    over.wait()


def finish(partial, squares):
    dma = pltpu.SemaphoreType.DMA
    return pl.pallas_call(
        finish_kernel,
        out_shape=jax.ShapeDtypeStruct((TB_DEV, BLK), jnp.float32),
        in_specs=[VMEM, VMEM],
        out_specs=VMEM,
        scratch_shapes=[pltpu.VMEM((NX, HALF, BLK), jnp.float32), dma((2,)), dma((2,))],
        compiler_params=pltpu.CompilerParams(collective_id=2, has_side_effects=True),
        name="finish",
    )(partial, squares)


def on_device(x_src, w_src, y_tgt, g_in, support_owner, support_local, live_count):
    core = lax.axis_index("core")
    live = lax.broadcasted_iota(jnp.int32, (RB_DEV, KH), 1) < live_count[0][:, None]
    listed = jnp.where(live, support_owner[0] * HALF + support_local[0], -1)
    g_half = lax.dynamic_slice_in_dim(g_in.reshape(TB_DEV, BLK), core * HALF, HALF, 0)
    x_all, y_all, bias_all, squares, items = gather(
        x_src, y_tgt, g_half, listed.reshape(1, RB_DEV * KH)
    )
    partial = local_call(
        row_kernel, ROWS, [pltpu.VMEM((5, ROWS, BLK), jnp.float32)], "rows"
    )(items, x_all, y_all, bias_all.reshape(NX * HALF, BLK))
    f_new, bias_rows = exchange(
        partial.reshape(NC * LINES, HALF_RB, BLK), w_src.reshape(RB_DEV, BLK), squares[:HALF_RB]
    )
    col = local_call(
        column_kernel,
        NX * HALF,
        [pltpu.VMEM((136, BLK), jnp.float32), pltpu.VMEM((136, BLK), jnp.float32)],
        "columns",
    )(items, x_all, y_all, bias_rows.reshape(ROWS, BLK))
    g_new = finish(col.reshape(NX, HALF, BLK), squares[HALF_RB:])
    return f_new.reshape(RB_DEV * BLK), g_new.reshape(TB_DEV * BLK)


def solution(mesh):
    fine = Mesh(mesh.devices.reshape(NX, NZ, NY, NC), ("x", "z", "y", "core"))
    src = ("x", "z", "y")
    placed = (
        P(None, src),
        P(src),
        P(None, src),
        P(src),
        P("core", src, None),
        P("core", src, None),
        P("core", src),
    )
    return jax.shard_map(
        on_device, mesh=fine, in_specs=placed, out_specs=(P(src), P(src)), check_vma=False
    )
```

```python
import functools
import heapq

import jax
import jax.numpy as jnp
import numpy as np
from jax import lax
from jax.experimental import pallas as pl
from jax.experimental.pallas import tpu as pltpu
from jax.sharding import Mesh, PartitionSpec as P

DIM = 64
BLK = 256
KH = 8
RB_DEV = 16
TB_DEV = 64
HALF = TB_DEV // 2

EPSILON = 0.1
EMPTY = -1e30
PER = 2.0 / (DIM * EPSILON)
PER2 = PER * float(np.log2(np.e))
OFFSET = DIM / 2.0
LN2 = float(np.log(2.0))
AUG = 16

MESH = pl.DeviceIdType.MESH
NX, NZ, NY, NC = 4, 8, 4, 2
LINES = NZ * NY
HALF_RB = RB_DEV // 2
ROWS = LINES * HALF_RB
NONE = NX * TB_DEV
STRIDE = 2 * NONE
MOST = LINES * 2 * NX * NC
WIDE = RB_DEV * KH
X_LANES = HALF_RB * BLK
Y_LANES = HALF * BLK
UNROLL = 8


def split3(row):
    high = row.astype(jnp.bfloat16).astype(jnp.float32)
    middle = (row - high).astype(jnp.bfloat16).astype(jnp.float32)
    low = row - high - middle
    at = lax.broadcasted_iota(jnp.int32, (AUG, BLK), 0)
    rows = jnp.where(at == 0, high, jnp.where(at == 1, middle, jnp.where(at == 2, low, 0.0)))
    return rows.astype(jnp.bfloat16)


def three_ones():
    at = lax.broadcasted_iota(jnp.int32, (AUG, BLK), 0)
    return jnp.where(at < 3, 1.0, 0.0).astype(jnp.bfloat16)


def tile_logits(left, right):
    return lax.dot_general(
        left, right, (((0,), (0,)), ((), ())), preferred_element_type=jnp.float32
    )


def peak_and_mass(tile):
    peak = jnp.max(tile, axis=0, keepdims=True)
    mass = jnp.sum(jnp.exp2((tile - peak) * PER2), axis=0, keepdims=True)
    return peak, mass


def lane_block(index):
    return pl.ds(pl.multiple_of(index * BLK, BLK), BLK)


def x_tile(x_ref, block):
    return x_ref[block // HALF_RB, :, lane_block(block % HALF_RB)]


def y_tile(y_ref, block):
    return y_ref[block // TB_DEV, :, lane_block(block % TB_DEV)]


def for_pairs(items_ref, visit):
    def step(group, carry):
        for k in range(UNROLL):
            code = items_ref[0, group * UNROLL + k]
            visit(code // STRIDE, code % STRIDE)
        return carry

    lax.fori_loop(0, (items_ref[1, 0] + UNROLL - 1) // UNROLL, step, 0)


def row_kernel(items_ref, x_ref, y_ref, bias_ref, out_ref, slots):
    slots[...] = jnp.full(slots.shape, EMPTY, jnp.float32)
    ones = three_ones()

    def visit(row, col):
        safe = col % NONE
        left = jnp.concatenate(
            [y_tile(y_ref, safe), split3(bias_ref[pl.ds(safe, 1), :])], axis=0
        )
        right = jnp.concatenate([x_tile(x_ref, row), ones], axis=0)
        peak, mass = peak_and_mass(tile_logits(left, right))
        slots[col // HALF, pl.ds(row, 1), :] = peak * PER2 + jnp.log2(mass)

    for_pairs(items_ref, visit)
    out_ref[...] = merged([slots[k] for k in range(NC * NX)])


def column_kernel(items_ref, x_ref, y_ref, bias_ref, out_ref, peaks, masses):
    peaks[...] = jnp.full(peaks.shape, EMPTY, jnp.float32)
    masses[...] = jnp.zeros(masses.shape, jnp.float32)
    ones = three_ones()

    def visit(row, col):
        left = jnp.concatenate(
            [x_tile(x_ref, row), split3(bias_ref[pl.ds(row, 1), :])], axis=0
        )
        right = jnp.concatenate([y_tile(y_ref, col % NONE), ones], axis=0)
        peak, mass = peak_and_mass(tile_logits(left, right))
        old = peaks[pl.ds(col, 1), :]
        new = jnp.maximum(old, peak)
        peaks[pl.ds(col, 1), :] = new
        masses[pl.ds(col, 1), :] = masses[pl.ds(col, 1), :] * jnp.exp2(
            (old - new) * PER2
        ) + mass * jnp.exp2((peak - new) * PER2)

    for_pairs(items_ref, visit)
    mass = masses[0:NONE, :]
    out_ref[...] = jnp.where(mass > 0.0, peaks[0:NONE, :] * PER2 + jnp.log2(mass), EMPTY)


SMEM = pl.BlockSpec(memory_space=pltpu.SMEM)
VMEM = pl.BlockSpec(memory_space=pltpu.VMEM)


def local_call(body, out_rows, scratch, name):
    return pl.pallas_call(
        body,
        out_shape=jax.ShapeDtypeStruct((out_rows, BLK), jnp.float32),
        in_specs=[SMEM, VMEM, VMEM, VMEM],
        out_specs=VMEM,
        scratch_shapes=scratch,
        compiler_params=pltpu.CompilerParams(vmem_limit_bytes=26 * 1024 * 1024),
        name=name,
    )


A_LANES = 3 * BLK
B_LANES = X_LANES - A_LANES
Y_CHUNKS = 4
CHUNK = Y_LANES // Y_CHUNKS


def anywhere():
    return pl.BlockSpec(memory_space=pl.ANY)


def place():
    return tuple(lax.axis_index(axis) for axis in ("x", "z", "y", "core"))


def moved(size, offset):
    longest = {8: 4, 4: 2}[size]
    shortest = size - 1 - longest
    out = []
    if -longest < offset <= 0:
        out.append((1, offset - 1))
    if 0 <= offset < shortest:
        out.append((-1, offset + 1))
    return out


def onward(piece):
    kind, a, b = piece
    if kind == "A":
        found = [("z", d, ("A", n, b)) for d, n in moved(NZ, a)]
        if a == 0:
            found += [("y", d, ("A", 0, n)) for d, n in moved(NY, b)]
    elif kind == "B":
        found = [("z", d, ("B", n, 0)) for d, n in moved(NZ, a)] if b == 0 else []
        found += [("y", d, ("B", a, n)) for d, n in moved(NY, b)]
    else:
        found = [("x", d, (kind, n, 0)) for d, n in moved(NX, a)]
    return found


def gather_plan():
    took = {"A": 2.0, "B": 2.0 * B_LANES / A_LANES, "Y": 2.0 * CHUNK / A_LANES}
    kinds = [f"Y{k}" for k in range(Y_CHUNKS)]
    first = [("B", 0, 0), ("A", 0, 0)] + [(k, 0, 0) for k in kinds]
    free, waiting, order = {}, [], []

    def send(now, piece):
        for axis, direction, seen in onward(piece):
            begin = max(now, free.get((axis, direction), 0.0))
            end = begin + took[piece[0][0]]
            free[axis, direction] = end
            heapq.heappush(waiting, (end + 1.0, seen))

    for piece in first:
        send(0.0, piece)
    while waiting:
        now, piece = heapq.heappop(waiting)
        order.append(piece)
        send(now, piece)
    return first, order


def gather_kernel(
    x_ref, y_ref, g_ref, owner_ref, local_ref, live_ref,
    x_all, y_all, bias_all, squares_ref, items_ref,
    codes, x_own, y_own, bias_sem, code_sem, own_sem, keep_sem, x_send, y_send, pair_sem, got,
):
    x, z, y, c = place()
    turn = 1 - 2 * c
    line = z * NY + y
    group = LINES * NC
    me = line * NC + c
    first, order = gather_plan()
    index = {piece: k for k, piece in enumerate(order)}

    barrier = pltpu.get_barrier_semaphore()
    sibling = (x, z, y, 1 - c)

    def plane_peer(k):
        other = lax.rem(me + k, group)
        return (x, other // (NY * NC), (other // NC) % NY, other % NC)

    def greet(k, carry):
        pl.semaphore_signal(barrier, inc=1, device_id=plane_peer(k), device_id_type=MESH)
        return carry

    line_peers = [(lax.rem(x + k, NX), z, y, core) for k in range(1, NX) for core in range(NC)]
    for device in line_peers:
        pl.semaphore_signal(barrier, inc=1, device_id=device, device_id_type=MESH)
    lax.fori_loop(1, group, greet, 0)

    x_mine = pl.multiple_of(c * X_LANES, X_LANES)
    y_mine = pl.multiple_of(c * Y_LANES, Y_LANES)
    owns = [
        pltpu.make_async_copy(x_ref.at[:, pl.ds(x_mine, X_LANES)], x_own, own_sem.at[0]),
        pltpu.make_async_copy(y_ref.at[:, pl.ds(y_mine, Y_LANES)], y_own, own_sem.at[1]),
    ]
    keeps = [
        pltpu.make_async_copy(
            x_ref.at[:, pl.ds(x_mine, X_LANES)], x_all.at[line], keep_sem.at[0]
        ),
        pltpu.make_async_copy(y_ref, y_all.at[x], keep_sem.at[1]),
    ]
    for copy in owns + keeps:
        copy.start()

    exact = functools.partial(
        jnp.dot, preferred_element_type=jnp.float32, precision=lax.Precision.HIGHEST
    )
    down, over = (lax.broadcasted_iota(jnp.int32, (RB_DEV, KH), k) for k in range(2))
    live = jnp.zeros((RB_DEV, KH), jnp.int32)
    for r in range(RB_DEV):
        live = jnp.where(down == r, live_ref[0, r], live)
    listed = jnp.where(over < live, owner_ref[0] * HALF + local_ref[0], -1).astype(jnp.float32)
    down, over = (lax.broadcasted_iota(jnp.int32, (KH, WIDE), k) for k in range(2))
    spread = exact(listed, (over % KH == down).astype(jnp.float32))
    down, over = (lax.broadcasted_iota(jnp.int32, (RB_DEV, WIDE), k) for k in range(2))
    codes[me] = jnp.sum(
        jnp.where(over // KH == down, spread, 0.0), axis=0, keepdims=True
    ).astype(jnp.int32)
    pl.semaphore_wait(barrier, group - 1 + len(line_peers))

    def lanes_of(kind):
        if kind == "A":
            return 0, A_LANES
        if kind == "B":
            return A_LANES, B_LANES
        return int(kind[1:]) * CHUNK, CHUNK

    def slot(piece):
        kind, a, b = piece
        begin, width = lanes_of(kind)
        if kind[0] == "Y":
            there = pl.ds(pl.multiple_of(y_mine + begin, BLK), width)
            return y_all.at[lax.rem(x + turn * a + NX, NX), :, there]
        origin = lax.rem(z + turn * a + NZ, NZ) * NY + lax.rem(y + turn * b + NY, NY)
        return x_all.at[origin, :, pl.ds(begin, width)]

    def source(piece):
        kind, a, b = piece
        if a or b:
            return slot(piece)
        begin, width = lanes_of(kind)
        if kind[0] == "Y":
            return y_ref.at[:, pl.ds(pl.multiple_of(y_mine + begin, BLK), width)]
        return x_ref.at[:, pl.ds(pl.multiple_of(x_mine + begin, BLK), width)]

    def neighbour(axis, direction):
        step = turn * direction
        return (
            lax.rem(x + step + NX, NX) if axis == "x" else x,
            lax.rem(z + step + NZ, NZ) if axis == "z" else z,
            lax.rem(y + step + NY, NY) if axis == "y" else y,
            c,
        )

    def pass_on(piece):
        for axis, direction, seen in onward(piece):
            pltpu.make_async_remote_copy(
                src_ref=source(piece),
                dst_ref=slot(piece),
                send_sem=y_send if piece[0][0] == "Y" else x_send,
                recv_sem=got.at[index[seen]],
                device_id=neighbour(axis, direction),
                device_id_type=MESH,
            ).start()

    for piece in first:
        pass_on(piece)

    def send_codes(k, carry):
        pltpu.make_async_remote_copy(
            src_ref=codes.at[me],
            dst_ref=codes.at[me],
            send_sem=code_sem.at[0],
            recv_sem=code_sem.at[1],
            device_id=plane_peer(k),
            device_id_type=MESH,
        ).start()
        return carry

    lax.fori_loop(1, group, send_codes, 0)

    def squares_of(tile):
        return 0.5 * jnp.sum(jnp.square(tile.astype(jnp.float32)), axis=0, keepdims=True)

    def do_x_squares():
        owns[0].wait()
        for k in range(HALF_RB):
            squares_ref[k : k + 1, :] = squares_of(x_own[:, k * BLK : (k + 1) * BLK])
        owns[1].wait()

    def do_y_squares(begin):
        for k in range(begin, begin + 8):
            squares_ref[HALF_RB + k : HALF_RB + k + 1, :] = squares_of(
                y_own[:, k * BLK : (k + 1) * BLK]
            )

    def do_bias():
        g_half = jnp.where(c == 0, g_ref[:HALF, :], g_ref[HALF:, :])
        here = bias_all.at[x * NC + c]
        here[...] = OFFSET * g_half.astype(jnp.float32) - squares_ref[HALF_RB:, :]
        for device in line_peers + [sibling]:
            pltpu.make_async_remote_copy(
                src_ref=here,
                dst_ref=here,
                send_sem=bias_sem.at[0],
                recv_sem=bias_sem.at[1],
                device_id=device,
                device_id_type=MESH,
            ).start()

    table = {}
    steps = 4

    def do_table():
        for side in range(2):
            most = codes.at[pl.ds(0, group - 1)]
            pltpu.make_async_copy(most, most, code_sem.at[side]).wait()
        halves = [codes[pl.ds(k, LINES, stride=NC)].reshape(LINES, WIDE) for k in range(NC)]
        lane = lax.broadcasted_iota(jnp.int32, (LINES, WIDE), 1)
        turned = [pltpu.roll(part, WIDE // 2, 1) for part in halves]
        even = jnp.where(lane < WIDE // 2, halves[0], turned[1])
        odd = jnp.where(lane < WIDE // 2, turned[0], halves[1])
        entry = jnp.where(c == 0, even, odd)
        owner = entry // HALF
        match = (entry >= 0) & (owner % LINES == line)
        row = (
            lax.broadcasted_iota(jnp.int32, entry.shape, 0) * HALF_RB
            + lane % (WIDE // 2) // KH
        )
        col = owner // LINES * TB_DEV + lane // (WIDE // 2) * HALF + entry % HALF
        hits = match.astype(jnp.float32)
        down, over = (lax.broadcasted_iota(jnp.int32, (WIDE, WIDE), k) for k in range(2))
        left = exact(hits, (down < over).astype(jnp.float32))
        totals = exact(hits, jnp.ones((WIDE, WIDE), jnp.float32))
        down, over = (lax.broadcasted_iota(jnp.int32, (LINES, LINES), k) for k in range(2))
        above = exact((over < down).astype(jnp.float32), totals)
        table["code"] = (row * STRIDE + col).astype(jnp.float32)
        table["spot"] = jnp.where(match, left + above, -1.0)
        table["count"] = jnp.sum(totals, axis=0, keepdims=True)
        table["found"] = jnp.zeros((MOST, WIDE), jnp.float32)

    def do_find(begin):
        spots = lax.broadcasted_iota(jnp.int32, (MOST, WIDE), 0).astype(jnp.float32)
        for k in range(begin, begin + LINES // steps):
            row = slice(k, k + 1)
            table["found"] += jnp.where(table["spot"][row] == spots, table["code"][row], 0.0)

    def do_items():
        items = lax.dot_general(
            jnp.ones((8, WIDE), jnp.float32),
            table["found"],
            (((1,), (1,)), ((), ())),
            preferred_element_type=jnp.float32,
            precision=lax.Precision.HIGHEST,
        )
        many = jnp.concatenate([table["count"]] * (MOST // WIDE), axis=1)
        spot = lax.broadcasted_iota(jnp.int32, (8, MOST), 1).astype(jnp.float32)
        items = jnp.where(spot < many, items, float(NONE))
        at = lax.broadcasted_iota(jnp.int32, (8, MOST), 0)
        items_ref[...] = jnp.where(at == 0, items, many).astype(jnp.int32)

    work = [do_x_squares]
    work += [functools.partial(do_y_squares, k) for k in range(0, HALF, 8)]
    work += [do_bias, do_table]
    work += [functools.partial(do_find, k) for k in range(0, LINES, LINES // steps)]
    work += [do_items]
    for at, piece in enumerate(order):
        here = slot(piece)
        pltpu.make_async_copy(here, here, got.at[index[piece]]).wait()
        pass_on(piece)
        if piece[0][0] == "Y":
            pltpu.make_async_remote_copy(
                src_ref=here,
                dst_ref=here,
                send_sem=pair_sem.at[0],
                recv_sem=pair_sem.at[1],
                device_id=sibling,
                device_id_type=MESH,
            ).start()
        if at % 3 == 0 and work:
            work.pop(0)()
    while work:
        work.pop(0)()

    for copy in keeps:
        copy.wait()
    most = x_all.at[pl.ds(0, LINES - 1)]
    pltpu.make_async_copy(most, most, x_send).wait()
    most = y_all.at[pl.ds(0, NX - 1), :, pl.ds(0, Y_LANES)]
    for semaphore in (y_send, pair_sem.at[0], pair_sem.at[1]):
        pltpu.make_async_copy(most, most, semaphore).wait()
    most = bias_all.at[pl.ds(0, NX * NC - 1)]
    for side in range(2):
        pltpu.make_async_copy(most, most, bias_sem.at[side]).wait()


def gather(x_src, y_tgt, g_rows, owners, locals_, lives):
    count = len(gather_plan()[1])
    dma = pltpu.SemaphoreType.DMA
    hbm = pl.BlockSpec(memory_space=pltpu.HBM)
    return pl.pallas_call(
        gather_kernel,
        out_shape=(
            pltpu.VMEM((LINES, DIM, X_LANES), jnp.bfloat16),
            pltpu.VMEM((NX, DIM, NC * Y_LANES), jnp.bfloat16),
            jax.ShapeDtypeStruct((NX * NC, HALF, BLK), jnp.float32),
            jax.ShapeDtypeStruct((HALF_RB + HALF, BLK), jnp.float32),
            jax.ShapeDtypeStruct((8, MOST), jnp.int32),
        ),
        in_specs=[hbm, hbm, VMEM, VMEM, VMEM, SMEM],
        out_specs=(VMEM, VMEM, VMEM, VMEM, VMEM),
        scratch_shapes=[
            pltpu.VMEM((LINES * NC, 1, WIDE), jnp.int32),
            pltpu.VMEM((DIM, X_LANES), jnp.bfloat16),
            pltpu.VMEM((DIM, Y_LANES), jnp.bfloat16),
            dma((2,)),
            dma((2,)),
            dma((2,)),
            dma((2,)),
            dma,
            dma,
            dma((2,)),
            dma((count,)),
        ],
        compiler_params=pltpu.CompilerParams(
            collective_id=0, has_side_effects=True, vmem_limit_bytes=26 * 1024 * 1024
        ),
        name="gather",
    )(x_src, y_tgt, g_rows, owners, locals_, lives)


def potential(logit2):
    logit = logit2 * LN2
    top = jnp.maximum(logit, 0.0)
    return -EPSILON * (top + jnp.log(jnp.exp(-top) + jnp.exp(logit - top)))


def merged(parts):
    top = functools.reduce(jnp.maximum, parts)
    return top + jnp.log2(sum(jnp.exp2(part - top) for part in parts))


def exchange_kernel(
    part_ref, w_ref, squares_ref, f_ref, bias_ref, parts, part_sem, bias_sem, f_sem
):
    x, z, y, c = place()
    group = LINES
    me = z * NY + y

    def peer(k):
        other = lax.rem(me + k, group)
        return other, (x, other // NY, other % NY, c)

    barrier = pltpu.get_barrier_semaphore()

    def greet(k, carry):
        pl.semaphore_signal(barrier, inc=1, device_id=peer(k)[1], device_id_type=MESH)
        return carry

    sibling = (x, z, y, 1 - c)
    pl.semaphore_signal(barrier, inc=1, device_id=sibling, device_id_type=MESH)
    lax.fori_loop(1, group, greet, 0)
    pl.semaphore_wait(barrier, group)

    def send_part(k, carry):
        other, device = peer(k)
        pltpu.make_async_remote_copy(
            src_ref=part_ref.at[other],
            dst_ref=parts.at[me],
            send_sem=part_sem.at[0],
            recv_sem=part_sem.at[1],
            device_id=device,
            device_id_type=MESH,
        ).start()
        return carry

    lax.fori_loop(1, group, send_part, 0)
    parts[me] = part_ref[me]
    others = parts.at[pl.ds(0, group - 1)]
    pltpu.make_async_copy(others, others, part_sem.at[1]).wait()
    squares = squares_ref[...]
    f_half = potential(merged([parts[k] for k in range(group)]) - PER2 * squares)
    mine = pl.ds(pl.multiple_of(c * HALF_RB, HALF_RB), HALF_RB)
    f_ref[mine, :] = f_half
    bias_ref[me] = OFFSET * f_half + (EPSILON * OFFSET) * w_ref[mine, :] - squares

    def send_bias(k, carry):
        pltpu.make_async_remote_copy(
            src_ref=bias_ref.at[me],
            dst_ref=bias_ref.at[me],
            send_sem=bias_sem.at[0],
            recv_sem=bias_sem.at[1],
            device_id=peer(k)[1],
            device_id_type=MESH,
        ).start()
        return carry

    lax.fori_loop(1, group, send_bias, 0)
    over = pltpu.make_async_remote_copy(
        src_ref=f_ref.at[mine, :],
        dst_ref=f_ref.at[mine, :],
        send_sem=f_sem.at[0],
        recv_sem=f_sem.at[1],
        device_id=sibling,
        device_id_type=MESH,
    )
    over.start()
    pltpu.make_async_copy(others, others, part_sem.at[0]).wait()
    others = bias_ref.at[pl.ds(0, group - 1)]
    for side in range(2):
        pltpu.make_async_copy(others, others, bias_sem.at[side]).wait()
    over.wait()


def exchange(partial, w_rows, squares):
    dma = pltpu.SemaphoreType.DMA
    group = LINES
    return pl.pallas_call(
        exchange_kernel,
        out_shape=(
            jax.ShapeDtypeStruct((RB_DEV, BLK), jnp.float32),
            jax.ShapeDtypeStruct((group, HALF_RB, BLK), jnp.float32),
        ),
        in_specs=[VMEM, VMEM, VMEM],
        out_specs=(VMEM, VMEM),
        scratch_shapes=[
            pltpu.VMEM((group, HALF_RB, BLK), jnp.float32),
            dma((2,)),
            dma((2,)),
            dma((2,)),
        ],
        compiler_params=pltpu.CompilerParams(
            collective_id=1, has_side_effects=True, vmem_limit_bytes=16 * 1024 * 1024
        ),
        name="exchange",
    )(partial, w_rows, squares)


def finish_kernel(part_ref, squares_ref, g_ref, parts, part_sem, g_sem):
    x, z, y, c = place()
    barrier = pltpu.get_barrier_semaphore()
    group = NX * NC
    me = x * NC + c
    peers = [lax.rem(me + k, group) for k in range(1, group)]
    sibling = (x, z, y, 1 - c)
    for other in peers:
        pl.semaphore_signal(
            barrier, inc=1, device_id=(other // NC, z, y, other % NC), device_id_type=MESH
        )
    pl.semaphore_wait(barrier, group - 1)
    for other in peers:
        pltpu.make_async_remote_copy(
            src_ref=part_ref.at[other],
            dst_ref=parts.at[me],
            send_sem=part_sem.at[0],
            recv_sem=part_sem.at[1],
            device_id=(other // NC, z, y, other % NC),
            device_id_type=MESH,
        ).start()
    parts[me] = part_ref[me]
    others = parts.at[pl.ds(0, group - 1)]
    pltpu.make_async_copy(others, others, part_sem.at[1]).wait()
    g_half = potential(merged([parts[k] for k in range(group)]) - PER2 * squares_ref[...])
    mine = pl.ds(pl.multiple_of(c * HALF, HALF), HALF)
    g_ref[mine, :] = g_half
    over = pltpu.make_async_remote_copy(
        src_ref=g_ref.at[mine, :],
        dst_ref=g_ref.at[mine, :],
        send_sem=g_sem.at[0],
        recv_sem=g_sem.at[1],
        device_id=sibling,
        device_id_type=MESH,
    )
    over.start()
    pltpu.make_async_copy(others, others, part_sem.at[0]).wait()
    over.wait()


def finish(partial, squares):
    dma = pltpu.SemaphoreType.DMA
    return pl.pallas_call(
        finish_kernel,
        out_shape=jax.ShapeDtypeStruct((TB_DEV, BLK), jnp.float32),
        in_specs=[VMEM, VMEM],
        out_specs=VMEM,
        scratch_shapes=[pltpu.VMEM((NX * NC, HALF, BLK), jnp.float32), dma((2,)), dma((2,))],
        compiler_params=pltpu.CompilerParams(
            collective_id=2, has_side_effects=True, vmem_limit_bytes=16 * 1024 * 1024
        ),
        name="finish",
    )(partial, squares)


def on_device(x_src, w_src, y_tgt, g_in, support_owner, support_local, live_count):
    x_all, y_all, bias_all, squares, items = gather(
        x_src, y_tgt, g_in.reshape(TB_DEV, BLK), support_owner, support_local, live_count
    )
    partial = local_call(
        row_kernel, ROWS, [pltpu.VMEM((NX * NC + 1, ROWS, BLK), jnp.float32)], "rows"
    )(items, x_all, y_all, bias_all.reshape(NONE, BLK))
    f_new, bias_rows = exchange(
        partial.reshape(LINES, HALF_RB, BLK), w_src.reshape(RB_DEV, BLK), squares[:HALF_RB]
    )
    col = local_call(
        column_kernel,
        NONE,
        [pltpu.VMEM((NONE + 8, BLK), jnp.float32), pltpu.VMEM((NONE + 8, BLK), jnp.float32)],
        "columns",
    )(items, x_all, y_all, bias_rows.reshape(ROWS, BLK))
    g_new = finish(col.reshape(NX * NC, HALF, BLK), squares[HALF_RB:])
    return f_new.reshape(RB_DEV * BLK), g_new.reshape(TB_DEV * BLK)


def solution(mesh):
    fine = Mesh(mesh.devices.reshape(NX, NZ, NY, NC), ("x", "z", "y", "core"))
    src = ("x", "z", "y")
    placed = (
        P(None, src),
        P(src),
        P(None, src),
        P(src),
        P("core", src, None),
        P("core", src, None),
        P("core", src),
    )
    return jax.shard_map(
        on_device, mesh=fine, in_specs=placed, out_specs=(P(src), P(src)), check_vma=False
    )
```

```python
import functools
import heapq

import jax
import jax.numpy as jnp
import numpy as np
from jax import lax
from jax.experimental import pallas as pl
from jax.experimental.pallas import tpu as pltpu
from jax.sharding import Mesh, PartitionSpec as P

DIM = 64
BLK = 256
KH = 8
RB_DEV = 16
TB_DEV = 64
HALF = TB_DEV // 2

EPSILON = 0.1
EMPTY = -1e30
PER = 2.0 / (DIM * EPSILON)
PER2 = PER * float(np.log2(np.e))
OFFSET = DIM / 2.0
LN2 = float(np.log(2.0))
AUG = 16

MESH = pl.DeviceIdType.MESH
NX, NZ, NY, NC = 4, 8, 4, 2
LINES = NZ * NY
HALF_RB = RB_DEV // 2
ROWS = LINES * HALF_RB
NONE = NX * TB_DEV
STRIDE = 2 * NONE
MOST = LINES * 2 * NX * NC
WIDE = RB_DEV * KH
X_LANES = HALF_RB * BLK
Y_LANES = HALF * BLK
UNROLL = 16
SAFE = 100.0


def extra_rows(row, at_left):
    high = row.astype(jnp.bfloat16).astype(jnp.float32)
    middle = (row - high).astype(jnp.bfloat16).astype(jnp.float32)
    low = row - high - middle
    at = lax.broadcasted_iota(jnp.int32, (AUG, BLK), 0)
    base = 0 if at_left else 3
    ones = jnp.where(at < 6, 1.0, 0.0)
    parts = jnp.where(at == base + 1, middle, jnp.where(at == base + 2, low, ones))
    return jnp.where(at == base, high, parts).astype(jnp.bfloat16)


def squares_of(tile):
    return 0.5 * jnp.sum(jnp.square(tile.astype(jnp.float32)), axis=0, keepdims=True)


def log2_mass(mass):
    return jnp.maximum(jnp.log2(mass), EMPTY)


def tile_logits(left, right):
    return lax.dot_general(
        left, right, (((0,), (0,)), ((), ())), preferred_element_type=jnp.float32
    )


def peak_and_mass(tile):
    peak = jnp.max(tile, axis=0, keepdims=True)
    mass = jnp.sum(jnp.exp2((tile - peak) * PER2), axis=0, keepdims=True)
    return peak, mass


def lane_block(index):
    return pl.ds(pl.multiple_of(index * BLK, BLK), BLK)


def x_tile(x_ref, block):
    return x_ref[block // HALF_RB, :, lane_block(block % HALF_RB)]


def y_tile(y_ref, block):
    return y_ref[block // TB_DEV, :, lane_block(block % TB_DEV)]


def for_pairs(items_ref, visit):
    def step(group, carry):
        for k in range(UNROLL):
            code = items_ref[0, group * UNROLL + k]
            visit(code // STRIDE, code % STRIDE)
        return carry

    lax.fori_loop(0, (items_ref[1, 0] + UNROLL - 1) // UNROLL, step, 0)


def plain_mass(tile):
    return jnp.sum(jnp.exp2(tile * PER2), axis=0, keepdims=True)


def one_of(col):
    return col // HALF, pl.ds(col % HALF, 1)


def row_kernel(items_ref, x_ref, y_ref, info_ref, out_ref, slots, bias):
    bias[...] = info_ref[:, 0] - info_ref[:, 1]
    safe = jnp.max(info_ref[:, 0]) * PER2 <= SAFE

    def logits(row, col):
        half, at = one_of(col % NONE)
        left = jnp.concatenate(
            [y_tile(y_ref, col % NONE), extra_rows(bias[half, at, :], True)], axis=0
        )
        tile = x_tile(x_ref, row)
        right = jnp.concatenate([tile, extra_rows(-squares_of(tile), False)], axis=0)
        return tile_logits(left, right)

    @pl.when(safe)
    def _():
        slots[...] = jnp.zeros(slots.shape, jnp.float32)

        def visit(row, col):
            slots[col // HALF, pl.ds(row, 1), :] = plain_mass(logits(row, col))

        for_pairs(items_ref, visit)
        out_ref[...] = log2_mass(sum(slots[k] for k in range(NC * NX)))

    @pl.when(jnp.logical_not(safe))
    def _():
        slots[...] = jnp.full(slots.shape, EMPTY, jnp.float32)

        def visit(row, col):
            peak, mass = peak_and_mass(logits(row, col))
            slots[col // HALF, pl.ds(row, 1), :] = peak * PER2 + jnp.log2(mass)

        for_pairs(items_ref, visit)
        out_ref[...] = merged([slots[k] for k in range(NC * NX)])


def column_kernel(
    items_ref, x_ref, y_ref, info_ref, offset_ref, out_ref, peaks, masses
):
    masses[...] = jnp.zeros(masses.shape, jnp.float32)
    safe = jnp.max(offset_ref[...]) * PER2 <= SAFE

    def logits(row, col):
        half, at = one_of(col % NONE)
        tile = x_tile(x_ref, row)
        bias = offset_ref[pl.ds(row, 1), :] - squares_of(tile)
        left = jnp.concatenate([tile, extra_rows(bias, True)], axis=0)
        square = info_ref[half, 1, at, :]
        right = jnp.concatenate(
            [y_tile(y_ref, col % NONE), extra_rows(-square, False)], axis=0
        )
        return tile_logits(left, right)

    @pl.when(safe)
    def _():
        def visit(row, col):
            masses[pl.ds(col, 1), :] += plain_mass(logits(row, col))

        for_pairs(items_ref, visit)
        out_ref[...] = log2_mass(masses[0:NONE, :])

    @pl.when(jnp.logical_not(safe))
    def _():
        peaks[...] = jnp.full(peaks.shape, EMPTY, jnp.float32)

        def visit(row, col):
            peak, mass = peak_and_mass(logits(row, col))
            old = peaks[pl.ds(col, 1), :]
            new = jnp.maximum(old, peak)
            peaks[pl.ds(col, 1), :] = new
            masses[pl.ds(col, 1), :] = masses[pl.ds(col, 1), :] * jnp.exp2(
                (old - new) * PER2
            ) + mass * jnp.exp2((peak - new) * PER2)

        for_pairs(items_ref, visit)
        out_ref[...] = jnp.maximum(
            peaks[0:NONE, :] * PER2 + log2_mass(masses[0:NONE, :]), EMPTY
        )


SMEM = pl.BlockSpec(memory_space=pltpu.SMEM)
VMEM = pl.BlockSpec(memory_space=pltpu.VMEM)


def local_call(body, arrays, out_rows, scratch, name):
    return pl.pallas_call(
        body,
        out_shape=jax.ShapeDtypeStruct((out_rows, BLK), jnp.float32),
        in_specs=[SMEM] + [VMEM] * arrays,
        out_specs=VMEM,
        scratch_shapes=scratch,
        compiler_params=pltpu.CompilerParams(vmem_limit_bytes=26 * 1024 * 1024),
        name=name,
    )


FIRST = ("Bl", "Bh", "A")
PARTS = {"A": (0, 3, 1), "Bl": (3, 2, -1), "Bh": (5, 3, 1)}
Y_CHUNKS = 4
CHUNK = Y_LANES // Y_CHUNKS


def anywhere():
    return pl.BlockSpec(memory_space=pl.ANY)


def place():
    return tuple(lax.axis_index(axis) for axis in ("x", "z", "y", "core"))


def moved(size, offset):
    longest = {8: 4, 4: 2}[size]
    shortest = size - 1 - longest
    out = []
    if -longest < offset <= 0:
        out.append((1, offset - 1))
    if 0 <= offset < shortest:
        out.append((-1, offset + 1))
    return out


def way(kind):
    if kind in PARTS:
        return PARTS[kind][2]
    return -1 if kind[0] == "Y" and int(kind[1:]) % 2 else 1


def onward(piece):
    kind, a, b = piece
    if kind[0] == "A":
        found = [("z", d, (kind, n, b)) for d, n in moved(NZ, a)]
        if a == 0:
            found += [("y", d, (kind, 0, n)) for d, n in moved(NY, b)]
    elif kind[0] in "BC":
        found = [("z", d, (kind, n, 0)) for d, n in moved(NZ, a)] if b == 0 else []
        found += [("y", d, (kind, a, n)) for d, n in moved(NY, b)]
    else:
        found = [("x", d, (kind, n, 0)) for d, n in moved(NX, a)]
    return found


def gather_plan():
    took = {kind: part[1] * BLK for kind, part in PARTS.items()} | {"C": 4}
    kinds = [f"Y{k}" for k in range(Y_CHUNKS)]
    took |= {kind: CHUNK for kind in kinds}
    first = [(kind, 0, 0) for kind in ["C", *FIRST, *kinds]]
    free, waiting, order = {}, [], []

    def send(now, piece):
        for axis, direction, seen in onward(piece):
            link = (axis, direction * way(piece[0]))
            end = max(now, free.get(link, 0.0)) + took[piece[0]]
            free[link] = end
            heapq.heappush(waiting, (end + 384.0, seen))

    for piece in first:
        send(0.0, piece)
    while waiting:
        now, piece = heapq.heappop(waiting)
        order.append(piece)
        send(now, piece)
    return first, order


def gather_kernel(
    x_ref, y_ref, g_ref, owner_ref, local_ref, live_ref,
    x_all, y_all, info_all, items_ref,
    codes, y_own, info_sem, code_sem, code_send, own_sem, keep_sem, x_send, y_send, pair_sem, got,
):
    x, z, y, c = place()
    turn = 1 - 2 * c
    line = z * NY + y
    first, order = gather_plan()
    index = {piece: k for k, piece in enumerate(order)}

    barrier = pltpu.get_barrier_semaphore()
    sibling = (x, z, y, 1 - c)

    line_peers = [(lax.rem(x + k, NX), z, y, core) for k in range(1, NX) for core in range(NC)]
    near = [(x, lax.rem(z + k, NZ), y, c) for k in (1, NZ - 1)]
    near += [(x, z, lax.rem(y + k, NY), c) for k in (1, NY - 1)]
    near += [sibling] + line_peers
    for device in near:
        pl.semaphore_signal(barrier, inc=1, device_id=device, device_id_type=MESH)

    x_mine = pl.multiple_of(c * X_LANES, X_LANES)
    y_mine = pl.multiple_of(c * Y_LANES, Y_LANES)
    own = pltpu.make_async_copy(y_ref.at[:, pl.ds(y_mine, Y_LANES)], y_own, own_sem)
    keeps = [
        pltpu.make_async_copy(
            x_ref.at[:, pl.ds(x_mine, X_LANES)], x_all.at[line], keep_sem.at[0]
        ),
        pltpu.make_async_copy(y_ref, y_all.at[x], keep_sem.at[1]),
    ]
    for copy in [own] + keeps:
        copy.start()

    exact = functools.partial(
        jnp.dot, preferred_element_type=jnp.float32, precision=lax.Precision.HIGHEST
    )
    slot_at = lax.broadcasted_iota(jnp.int32, (KH, RB_DEV), 0)
    listed = owner_ref[0] * HALF + local_ref[0]
    listed = jnp.where(slot_at < live_ref[...], listed, -1).astype(jnp.float32)
    down, over = (lax.broadcasted_iota(jnp.int32, (RB_DEV, WIDE), k) for k in range(2))
    spread = exact(listed, (over // KH == down).astype(jnp.float32))
    down, over = (lax.broadcasted_iota(jnp.int32, (KH, WIDE), k) for k in range(2))
    codes[c, line] = jnp.sum(
        jnp.where(over % KH == down, spread, 0.0), axis=0, keepdims=True
    ).astype(jnp.int32)
    pl.semaphore_wait(barrier, len(near))

    def lanes_of(kind):
        if kind in PARTS:
            return PARTS[kind][0] * BLK, PARTS[kind][1] * BLK
        return int(kind[1:]) * CHUNK, CHUNK

    def slot(piece):
        kind, a, b = piece
        ahead = turn * way(kind)
        origin = lax.rem(z + ahead * a + NZ, NZ) * NY + lax.rem(y + ahead * b + NY, NY)
        if kind == "C":
            return codes.at[c, origin]
        begin, width = lanes_of(kind)
        if kind[0] == "Y":
            there = pl.ds(pl.multiple_of(y_mine + begin, BLK), width)
            return y_all.at[lax.rem(x + ahead * a + NX, NX), :, there]
        return x_all.at[origin, :, pl.ds(begin, width)]

    def source(piece):
        kind, a, b = piece
        if a or b or kind == "C":
            return slot(piece)
        begin, width = lanes_of(kind)
        if kind[0] == "Y":
            return y_ref.at[:, pl.ds(pl.multiple_of(y_mine + begin, BLK), width)]
        return x_ref.at[:, pl.ds(pl.multiple_of(x_mine + begin, BLK), width)]

    def neighbour(axis, direction):
        step = turn * direction
        return (
            lax.rem(x + step + NX, NX) if axis == "x" else x,
            lax.rem(z + step + NZ, NZ) if axis == "z" else z,
            lax.rem(y + step + NY, NY) if axis == "y" else y,
            c,
        )

    def pass_on(piece):
        for axis, direction, seen in onward(piece):
            pltpu.make_async_remote_copy(
                src_ref=source(piece),
                dst_ref=slot(piece),
                send_sem={"Y": y_send, "C": code_send}.get(piece[0][0], x_send),
                recv_sem=got.at[index[seen]],
                device_id=neighbour(axis, direction * way(piece[0])),
                device_id_type=MESH,
            ).start()

    for piece in first:
        pass_on(piece)

    info = info_all.at[x * NC + c]

    def do_y_squares(begin):
        if begin == 0:
            own.wait()
        for k in range(begin, begin + 8):
            info[1, k : k + 1, :] = squares_of(y_own[:, k * BLK : (k + 1) * BLK])

    def do_info():
        g_half = jnp.where(c == 0, g_ref[:HALF, :], g_ref[HALF:, :])
        info[0] = OFFSET * g_half.astype(jnp.float32)
        for device in line_peers + [sibling]:
            pltpu.make_async_remote_copy(
                src_ref=info,
                dst_ref=info,
                send_sem=info_sem.at[0],
                recv_sem=info_sem.at[1],
                device_id=device,
                device_id_type=MESH,
            ).start()

    def over_codes():
        return pltpu.make_async_remote_copy(
            src_ref=codes.at[c],
            dst_ref=codes.at[c],
            send_sem=code_sem.at[0],
            recv_sem=code_sem.at[1],
            device_id=sibling,
            device_id_type=MESH,
        )

    table = {}
    steps = 4

    def do_table():
        over_codes().wait()
        halves = [codes[k].reshape(LINES, WIDE) for k in range(NC)]
        lane = lax.broadcasted_iota(jnp.int32, (LINES, WIDE), 1)
        turned = [pltpu.roll(part, WIDE // 2, 1) for part in halves]
        even = jnp.where(lane < WIDE // 2, halves[0], turned[1])
        odd = jnp.where(lane < WIDE // 2, turned[0], halves[1])
        entry = jnp.where(c == 0, even, odd)
        owner = entry // HALF
        match = (entry >= 0) & (owner % LINES == line)
        row = (
            lax.broadcasted_iota(jnp.int32, entry.shape, 0) * HALF_RB
            + lane % (WIDE // 2) // KH
        )
        col = owner // LINES * TB_DEV + lane // (WIDE // 2) * HALF + entry % HALF
        hits = match.astype(jnp.float32)
        down, over = (lax.broadcasted_iota(jnp.int32, (WIDE, WIDE), k) for k in range(2))
        left = exact(hits, (down < over).astype(jnp.float32))
        totals = exact(hits, jnp.ones((WIDE, WIDE), jnp.float32))
        down, over = (lax.broadcasted_iota(jnp.int32, (LINES, LINES), k) for k in range(2))
        above = exact((over < down).astype(jnp.float32), totals)
        table["code"] = (row * STRIDE + col).astype(jnp.float32)
        table["spot"] = jnp.where(match, left + above, -1.0)
        table["count"] = jnp.sum(totals, axis=0, keepdims=True)
        table["found"] = jnp.zeros((MOST, WIDE), jnp.float32)

    def do_find(begin):
        spots = lax.broadcasted_iota(jnp.int32, (MOST, WIDE), 0).astype(jnp.float32)
        for k in range(begin, begin + LINES // steps):
            row = slice(k, k + 1)
            table["found"] += jnp.where(table["spot"][row] == spots, table["code"][row], 0.0)

    def do_items():
        items = lax.dot_general(
            jnp.ones((8, WIDE), jnp.float32),
            table["found"],
            (((1,), (1,)), ((), ())),
            preferred_element_type=jnp.float32,
            precision=lax.Precision.HIGHEST,
        )
        many = jnp.concatenate([table["count"]] * (MOST // WIDE), axis=1)
        spot = lax.broadcasted_iota(jnp.int32, (8, MOST), 1).astype(jnp.float32)
        items = jnp.where(spot < many, items, float(NONE))
        at = lax.broadcasted_iota(jnp.int32, (8, MOST), 0)
        items_ref[...] = jnp.where(at == 0, items, many).astype(jnp.int32)

    early = [functools.partial(do_y_squares, k) for k in range(0, HALF, 8)]
    early += [do_info]
    late = [do_table]
    late += [functools.partial(do_find, k) for k in range(0, LINES, LINES // steps)]
    late += [do_items]
    codes_left, between = LINES - 1, 0
    for piece in order:
        here = slot(piece)
        pltpu.make_async_copy(here, here, got.at[index[piece]]).wait()
        pass_on(piece)
        if piece[0] == "C":
            codes_left -= 1
            if codes_left == 0:
                over_codes().start()
            continue
        if piece[0][0] == "Y":
            pltpu.make_async_remote_copy(
                src_ref=here,
                dst_ref=here,
                send_sem=pair_sem.at[0],
                recv_sem=pair_sem.at[1],
                device_id=sibling,
                device_id_type=MESH,
            ).start()
        between += 1
        if between % 3 == 0:
            if early:
                early.pop(0)()
            elif late and codes_left == 0:
                late.pop(0)()
    for task in early + late:
        task()

    for copy in keeps:
        copy.wait()
    most = x_all.at[pl.ds(0, LINES - 1)]
    pltpu.make_async_copy(most, most, x_send).wait()
    most = y_all.at[pl.ds(0, NX - 1), :, pl.ds(0, Y_LANES)]
    for semaphore in (y_send, pair_sem.at[0], pair_sem.at[1]):
        pltpu.make_async_copy(most, most, semaphore).wait()
    most = info_all.at[pl.ds(0, NX * NC - 1)]
    for side in range(2):
        pltpu.make_async_copy(most, most, info_sem.at[side]).wait()
    most = codes.at[0, pl.ds(0, LINES - 1)]
    pltpu.make_async_copy(most, most, code_send).wait()


def gather(x_src, y_tgt, g_rows, owners, locals_, lives):
    count = len(gather_plan()[1])
    dma = pltpu.SemaphoreType.DMA
    hbm = pl.BlockSpec(memory_space=pltpu.HBM)
    return pl.pallas_call(
        gather_kernel,
        out_shape=(
            pltpu.VMEM((LINES, DIM, X_LANES), jnp.bfloat16),
            pltpu.VMEM((NX, DIM, NC * Y_LANES), jnp.bfloat16),
            jax.ShapeDtypeStruct((NX * NC, 2, HALF, BLK), jnp.float32),
            jax.ShapeDtypeStruct((8, MOST), jnp.int32),
        ),
        in_specs=[hbm, hbm, VMEM, VMEM, VMEM, VMEM],
        out_specs=(VMEM, VMEM, VMEM, VMEM),
        scratch_shapes=[
            pltpu.VMEM((NC, LINES, 1, WIDE), jnp.int32),
            pltpu.VMEM((DIM, Y_LANES), jnp.bfloat16),
            dma((2,)),
            dma((2,)),
            dma,
            dma,
            dma((2,)),
            dma,
            dma,
            dma((2,)),
            dma((count,)),
        ],
        compiler_params=pltpu.CompilerParams(
            collective_id=0, has_side_effects=True, vmem_limit_bytes=26 * 1024 * 1024
        ),
        name="gather",
    )(x_src, y_tgt, g_rows, owners, locals_, lives)


def potential(logit2):
    logit = logit2 * LN2
    top = jnp.maximum(logit, 0.0)
    return -EPSILON * (top + jnp.log(jnp.exp(-top) + jnp.exp(logit - top)))


def merged(parts):
    top = functools.reduce(jnp.maximum, parts)
    return top + jnp.log2(sum(jnp.exp2(part - top) for part in parts))


def exchange_kernel(
    part_ref, w_ref, f_ref, bias_ref, parts, part_sem, bias_sem, f_sem
):
    x, z, y, c = place()
    group = LINES
    me = z * NY + y

    def peer(k):
        other = lax.rem(me + k, group)
        return other, (x, other // NY, other % NY, c)

    barrier = pltpu.get_barrier_semaphore()

    def greet(k, carry):
        pl.semaphore_signal(barrier, inc=1, device_id=peer(k)[1], device_id_type=MESH)
        return carry

    sibling = (x, z, y, 1 - c)
    pl.semaphore_signal(barrier, inc=1, device_id=sibling, device_id_type=MESH)
    lax.fori_loop(1, group, greet, 0)
    pl.semaphore_wait(barrier, group)

    def send_part(k, carry):
        other, device = peer(k)
        pltpu.make_async_remote_copy(
            src_ref=part_ref.at[other],
            dst_ref=parts.at[me],
            send_sem=part_sem.at[0],
            recv_sem=part_sem.at[1],
            device_id=device,
            device_id_type=MESH,
        ).start()
        return carry

    lax.fori_loop(1, group, send_part, 0)
    parts[me] = part_ref[me]
    others = parts.at[pl.ds(0, group - 1)]
    pltpu.make_async_copy(others, others, part_sem.at[1]).wait()
    f_half = potential(merged([parts[k] for k in range(group)]))
    mine = pl.ds(pl.multiple_of(c * HALF_RB, HALF_RB), HALF_RB)
    f_ref[mine, :] = f_half
    bias_ref[me] = OFFSET * f_half + (EPSILON * OFFSET) * w_ref[mine, :]

    def send_bias(k, carry):
        pltpu.make_async_remote_copy(
            src_ref=bias_ref.at[me],
            dst_ref=bias_ref.at[me],
            send_sem=bias_sem.at[0],
            recv_sem=bias_sem.at[1],
            device_id=peer(k)[1],
            device_id_type=MESH,
        ).start()
        return carry

    lax.fori_loop(1, group, send_bias, 0)
    over = pltpu.make_async_remote_copy(
        src_ref=f_ref.at[mine, :],
        dst_ref=f_ref.at[mine, :],
        send_sem=f_sem.at[0],
        recv_sem=f_sem.at[1],
        device_id=sibling,
        device_id_type=MESH,
    )
    over.start()
    pltpu.make_async_copy(others, others, part_sem.at[0]).wait()
    others = bias_ref.at[pl.ds(0, group - 1)]
    for side in range(2):
        pltpu.make_async_copy(others, others, bias_sem.at[side]).wait()
    over.wait()


def exchange(partial, w_rows):
    dma = pltpu.SemaphoreType.DMA
    group = LINES
    return pl.pallas_call(
        exchange_kernel,
        out_shape=(
            jax.ShapeDtypeStruct((RB_DEV, BLK), jnp.float32),
            jax.ShapeDtypeStruct((group, HALF_RB, BLK), jnp.float32),
        ),
        in_specs=[VMEM, VMEM],
        out_specs=(VMEM, VMEM),
        scratch_shapes=[
            pltpu.VMEM((group, HALF_RB, BLK), jnp.float32),
            dma((2,)),
            dma((2,)),
            dma((2,)),
        ],
        compiler_params=pltpu.CompilerParams(
            collective_id=1, has_side_effects=True, vmem_limit_bytes=16 * 1024 * 1024
        ),
        name="exchange",
    )(partial, w_rows)


def finish_kernel(part_ref, g_ref, parts, part_sem, g_sem):
    x, z, y, c = place()
    barrier = pltpu.get_barrier_semaphore()
    group = NX * NC
    me = x * NC + c
    peers = [lax.rem(me + k, group) for k in range(1, group)]
    sibling = (x, z, y, 1 - c)
    for other in peers:
        pl.semaphore_signal(
            barrier, inc=1, device_id=(other // NC, z, y, other % NC), device_id_type=MESH
        )
    pl.semaphore_wait(barrier, group - 1)
    for other in peers:
        pltpu.make_async_remote_copy(
            src_ref=part_ref.at[other],
            dst_ref=parts.at[me],
            send_sem=part_sem.at[0],
            recv_sem=part_sem.at[1],
            device_id=(other // NC, z, y, other % NC),
            device_id_type=MESH,
        ).start()
    parts[me] = part_ref[me]
    others = parts.at[pl.ds(0, group - 1)]
    pltpu.make_async_copy(others, others, part_sem.at[1]).wait()
    g_half = potential(merged([parts[k] for k in range(group)]))
    mine = pl.ds(pl.multiple_of(c * HALF, HALF), HALF)
    g_ref[mine, :] = g_half
    over = pltpu.make_async_remote_copy(
        src_ref=g_ref.at[mine, :],
        dst_ref=g_ref.at[mine, :],
        send_sem=g_sem.at[0],
        recv_sem=g_sem.at[1],
        device_id=sibling,
        device_id_type=MESH,
    )
    over.start()
    pltpu.make_async_copy(others, others, part_sem.at[0]).wait()
    over.wait()


def finish(partial):
    dma = pltpu.SemaphoreType.DMA
    return pl.pallas_call(
        finish_kernel,
        out_shape=jax.ShapeDtypeStruct((TB_DEV, BLK), jnp.float32),
        in_specs=[VMEM],
        out_specs=VMEM,
        scratch_shapes=[pltpu.VMEM((NX * NC, HALF, BLK), jnp.float32), dma((2,)), dma((2,))],
        compiler_params=pltpu.CompilerParams(
            collective_id=2, has_side_effects=True, vmem_limit_bytes=16 * 1024 * 1024
        ),
        name="finish",
    )(partial)


def on_device(x_src, w_src, y_tgt, g_in, support_owner, support_local, live_count):
    f32 = jnp.float32
    x_all, y_all, info, items = gather(
        pltpu.with_memory_space_constraint(x_src, pltpu.HBM),
        pltpu.with_memory_space_constraint(y_tgt, pltpu.HBM),
        g_in.reshape(TB_DEV, BLK),
        jnp.swapaxes(support_owner, 1, 2),
        jnp.swapaxes(support_local, 1, 2),
        live_count,
    )
    shared = (items, x_all, y_all, info)
    scratch = [pltpu.VMEM((NX * NC + 1, ROWS, BLK), f32), pltpu.VMEM((NX * NC, HALF, BLK), f32)]
    partial = local_call(row_kernel, 3, ROWS, scratch, "rows")(*shared)
    f_new, offsets = exchange(
        partial.reshape(LINES, HALF_RB, BLK), w_src.reshape(RB_DEV, BLK)
    )
    scratch = [pltpu.VMEM((NONE + 8, BLK), f32)] * 2
    col = local_call(column_kernel, 4, NONE, scratch, "columns")(
        *shared, offsets.reshape(ROWS, BLK)
    )
    g_new = finish(col.reshape(NX * NC, HALF, BLK))
    return f_new.reshape(RB_DEV * BLK), g_new.reshape(TB_DEV * BLK)


def solution(mesh):
    fine = Mesh(mesh.devices.reshape(NX, NZ, NY, NC), ("x", "z", "y", "core"))
    src = ("x", "z", "y")
    placed = (
        P(None, src),
        P(src),
        P(None, src),
        P(src),
        P("core", src, None),
        P("core", src, None),
        P("core", src),
    )
    return jax.shard_map(
        on_device, mesh=fine, in_specs=placed, out_specs=(P(src), P(src)), check_vma=False
    )
```

```python
import functools
import heapq

import jax
import jax.numpy as jnp
import numpy as np
from jax import lax
from jax.experimental import pallas as pl
from jax.experimental.pallas import tpu as pltpu
from jax.sharding import Mesh, PartitionSpec as P

DIM = 64
BLK = 256
KH = 8
RB_DEV = 16
TB_DEV = 64
HALF = TB_DEV // 2

EPSILON = 0.1
EMPTY = -1e30
PER = 2.0 / (DIM * EPSILON)
PER2 = PER * float(np.log2(np.e))
OFFSET = DIM / 2.0
LN2 = float(np.log(2.0))
AUG = 16

MESH = pl.DeviceIdType.MESH
NX, NZ, NY, NC = 4, 8, 4, 2
LINES = NZ * NY
HALF_RB = RB_DEV // 2
ROWS = LINES * HALF_RB
NONE = NX * TB_DEV
STRIDE = 2 * NONE
MOST = LINES * 2 * NX * NC
WIDE = RB_DEV * KH
X_LANES = HALF_RB * BLK
Y_LANES = HALF * BLK
UNROLL = 16
SAFE = 100.0


def extra_rows(row, at_left):
    high = row.astype(jnp.bfloat16).astype(jnp.float32)
    middle = (row - high).astype(jnp.bfloat16).astype(jnp.float32)
    low = row - high - middle
    at = lax.broadcasted_iota(jnp.int32, (AUG, BLK), 0)
    base = 0 if at_left else 3
    ones = jnp.where(at < 6, 1.0, 0.0)
    parts = jnp.where(at == base + 1, middle, jnp.where(at == base + 2, low, ones))
    return jnp.where(at == base, high, parts).astype(jnp.bfloat16)


def squares_of(tile):
    return 0.5 * jnp.sum(jnp.square(tile.astype(jnp.float32)), axis=0, keepdims=True)


def log2_mass(mass):
    return jnp.maximum(jnp.log2(mass), EMPTY)


def tile_logits(left, right):
    return lax.dot_general(
        left, right, (((0,), (0,)), ((), ())), preferred_element_type=jnp.float32
    )


def peak_and_mass(tile):
    peak = jnp.max(tile, axis=0, keepdims=True)
    mass = jnp.sum(jnp.exp2((tile - peak) * PER2), axis=0, keepdims=True)
    return peak, mass


def lane_block(index):
    return pl.ds(pl.multiple_of(index * BLK, BLK), BLK)


def x_tile(x_ref, block):
    return x_ref[block // HALF_RB, :, lane_block(block % HALF_RB)]


def y_tile(y_ref, block):
    return y_ref[block // TB_DEV, :, lane_block(block % TB_DEV)]


def for_pairs(items_ref, visit):
    def step(group, carry):
        for k in range(UNROLL):
            code = items_ref[0, group * UNROLL + k]
            visit(code // STRIDE, code % STRIDE)
        return carry

    lax.fori_loop(0, (items_ref[1, 0] + UNROLL - 1) // UNROLL, step, 0)


def plain_mass(tile):
    return jnp.sum(jnp.exp2(tile * PER2), axis=0, keepdims=True)


def one_of(col):
    return col // HALF, pl.ds(col % HALF, 1)


def row_kernel(items_ref, x_ref, y_ref, info_ref, out_ref, slots, bias):
    bias[...] = info_ref[:, 0] - info_ref[:, 1]
    safe = jnp.max(info_ref[:, 0]) * PER2 <= SAFE

    def logits(row, col):
        half, at = one_of(col % NONE)
        left = jnp.concatenate(
            [y_tile(y_ref, col % NONE), extra_rows(bias[half, at, :], True)], axis=0
        )
        tile = x_tile(x_ref, row)
        right = jnp.concatenate([tile, extra_rows(-squares_of(tile), False)], axis=0)
        return tile_logits(left, right)

    @pl.when(safe)
    def _():
        slots[...] = jnp.zeros(slots.shape, jnp.float32)

        def visit(row, col):
            slots[col // HALF, pl.ds(row, 1), :] = plain_mass(logits(row, col))

        for_pairs(items_ref, visit)
        out_ref[...] = log2_mass(sum(slots[k] for k in range(NC * NX)))

    @pl.when(jnp.logical_not(safe))
    def _():
        slots[...] = jnp.full(slots.shape, EMPTY, jnp.float32)

        def visit(row, col):
            peak, mass = peak_and_mass(logits(row, col))
            slots[col // HALF, pl.ds(row, 1), :] = peak * PER2 + jnp.log2(mass)

        for_pairs(items_ref, visit)
        out_ref[...] = merged([slots[k] for k in range(NC * NX)])


def column_kernel(
    items_ref, x_ref, y_ref, info_ref, offset_ref, out_ref, peaks, masses
):
    masses[...] = jnp.zeros(masses.shape, jnp.float32)
    safe = jnp.max(offset_ref[...]) * PER2 <= SAFE

    def logits(row, col):
        half, at = one_of(col % NONE)
        tile = x_tile(x_ref, row)
        bias = offset_ref[pl.ds(row, 1), :] - squares_of(tile)
        left = jnp.concatenate([tile, extra_rows(bias, True)], axis=0)
        square = info_ref[half, 1, at, :]
        right = jnp.concatenate(
            [y_tile(y_ref, col % NONE), extra_rows(-square, False)], axis=0
        )
        return tile_logits(left, right)

    @pl.when(safe)
    def _():
        def visit(row, col):
            masses[pl.ds(col, 1), :] += plain_mass(logits(row, col))

        for_pairs(items_ref, visit)
        out_ref[...] = log2_mass(masses[0:NONE, :])

    @pl.when(jnp.logical_not(safe))
    def _():
        peaks[...] = jnp.full(peaks.shape, EMPTY, jnp.float32)

        def visit(row, col):
            peak, mass = peak_and_mass(logits(row, col))
            old = peaks[pl.ds(col, 1), :]
            new = jnp.maximum(old, peak)
            peaks[pl.ds(col, 1), :] = new
            masses[pl.ds(col, 1), :] = masses[pl.ds(col, 1), :] * jnp.exp2(
                (old - new) * PER2
            ) + mass * jnp.exp2((peak - new) * PER2)

        for_pairs(items_ref, visit)
        out_ref[...] = jnp.maximum(
            peaks[0:NONE, :] * PER2 + log2_mass(masses[0:NONE, :]), EMPTY
        )


SMEM = pl.BlockSpec(memory_space=pltpu.SMEM)
VMEM = pl.BlockSpec(memory_space=pltpu.VMEM)


def local_call(body, arrays, out_rows, scratch, name):
    return pl.pallas_call(
        body,
        out_shape=jax.ShapeDtypeStruct((out_rows, BLK), jnp.float32),
        in_specs=[SMEM] + [VMEM] * arrays,
        out_specs=VMEM,
        scratch_shapes=scratch,
        compiler_params=pltpu.CompilerParams(vmem_limit_bytes=26 * 1024 * 1024),
        name=name,
    )


FIRST = ("Bl", "Bh", "A")
PARTS = {"A": (0, 768, 1), "Bl": (768, 512, -1), "Bh": (1280, 768, 1)}
Y_CHUNKS = 4
CHUNK = Y_LANES // Y_CHUNKS


def place():
    return tuple(lax.axis_index(axis) for axis in ("x", "z", "y", "core"))


def moved(size, offset):
    longest = {8: 4, 4: 2}[size]
    shortest = size - 1 - longest
    out = []
    if -longest < offset <= 0:
        out.append((1, offset - 1))
    if 0 <= offset < shortest:
        out.append((-1, offset + 1))
    return out


def way(kind):
    if kind in PARTS:
        return PARTS[kind][2]
    return -1 if kind[0] == "Y" and int(kind[1:]) % 2 else 1


def onward(piece):
    kind, a, b = piece
    if kind[0] == "A":
        found = [("z", d, (kind, n, b)) for d, n in moved(NZ, a)]
        if a == 0:
            found += [("y", d, (kind, 0, n)) for d, n in moved(NY, b)]
    elif kind[0] in "BC":
        found = [("z", d, (kind, n, 0)) for d, n in moved(NZ, a)] if b == 0 else []
        found += [("y", d, (kind, a, n)) for d, n in moved(NY, b)]
    else:
        found = [("x", d, (kind, n, 0)) for d, n in moved(NX, a)]
    return found


def gather_plan():
    took = {kind: part[1] for kind, part in PARTS.items()} | {"C": 4}
    kinds = [f"Y{k}" for k in range(Y_CHUNKS)]
    took |= {kind: CHUNK for kind in kinds}
    first = [(kind, 0, 0) for kind in ["C", *FIRST, *kinds]]
    free, waiting, order = {}, [], []

    def send(now, piece):
        for axis, direction, seen in onward(piece):
            link = (axis, direction * way(piece[0]))
            end = max(now, free.get(link, 0.0)) + took[piece[0]]
            free[link] = end
            heapq.heappush(waiting, (end + 384.0, seen))

    for piece in first:
        send(0.0, piece)
    while waiting:
        now, piece = heapq.heappop(waiting)
        order.append(piece)
        send(now, piece)
    return first, order


def gather_kernel(
    x_ref, y_ref, g_hbm, owner_hbm, local_hbm, live_hbm,
    x_all, y_all, info_all, items_ref,
    codes, y_own, g_ref, owner_ref, local_ref, live_ref, small_sem, info_sem, code_sem, code_send, own_sem, keep_sem, x_send, y_send, pair_sem, got,
):
    x, z, y, c = place()
    turn = 1 - 2 * c
    line = z * NY + y
    first, order = gather_plan()
    index = {piece: k for k, piece in enumerate(order)}

    small = [
        pltpu.make_async_copy(there, here, small_sem.at[k])
        for k, (there, here) in enumerate(
            [(owner_hbm, owner_ref), (local_hbm, local_ref), (live_hbm, live_ref), (g_hbm, g_ref)]
        )
    ]
    for copy in small:
        copy.start()
    barrier = pltpu.get_barrier_semaphore()
    sibling = (x, z, y, 1 - c)

    line_peers = [(lax.rem(x + k, NX), z, y, core) for k in range(1, NX) for core in range(NC)]
    near = [(x, lax.rem(z + k, NZ), y, c) for k in (1, NZ - 1)]
    near += [(x, z, lax.rem(y + k, NY), c) for k in (1, NY - 1)]
    near += [sibling] + line_peers
    for device in near:
        pl.semaphore_signal(barrier, inc=1, device_id=device, device_id_type=MESH)

    x_mine = pl.multiple_of(c * X_LANES, X_LANES)
    y_mine = pl.multiple_of(c * Y_LANES, Y_LANES)
    own = pltpu.make_async_copy(y_ref.at[:, pl.ds(y_mine, Y_LANES)], y_own, own_sem)
    keeps = [
        pltpu.make_async_copy(
            x_ref.at[:, pl.ds(x_mine, X_LANES)], x_all.at[line], keep_sem.at[0]
        ),
        pltpu.make_async_copy(y_ref, y_all.at[x], keep_sem.at[1]),
    ]
    for copy in [own] + keeps:
        copy.start()

    exact = functools.partial(
        jnp.dot, preferred_element_type=jnp.float32, precision=lax.Precision.HIGHEST
    )
    for copy in small:
        copy.wait()
    slot_at = lax.broadcasted_iota(jnp.int32, (KH, RB_DEV), 0)
    listed = owner_ref[0] * HALF + local_ref[0]
    listed = jnp.where(slot_at < live_ref[...], listed, -1).astype(jnp.float32)
    down, over = (lax.broadcasted_iota(jnp.int32, (RB_DEV, WIDE), k) for k in range(2))
    spread = exact(listed, (over // KH == down).astype(jnp.float32))
    down, over = (lax.broadcasted_iota(jnp.int32, (KH, WIDE), k) for k in range(2))
    codes[c, line] = jnp.sum(
        jnp.where(over % KH == down, spread, 0.0), axis=0, keepdims=True
    ).astype(jnp.int32)
    pl.semaphore_wait(barrier, len(near))

    def lanes_of(kind):
        if kind in PARTS:
            return PARTS[kind][:2]
        return int(kind[1:]) * CHUNK, CHUNK

    def slot(piece):
        kind, a, b = piece
        ahead = turn * way(kind)
        origin = lax.rem(z + ahead * a + NZ, NZ) * NY + lax.rem(y + ahead * b + NY, NY)
        if kind == "C":
            return codes.at[c, origin]
        begin, width = lanes_of(kind)
        if kind[0] == "Y":
            there = pl.ds(pl.multiple_of(y_mine + begin, BLK), width)
            return y_all.at[lax.rem(x + ahead * a + NX, NX), :, there]
        return x_all.at[origin, :, pl.ds(begin, width)]

    def source(piece):
        kind, a, b = piece
        if a or b or kind == "C":
            return slot(piece)
        begin, width = lanes_of(kind)
        if kind[0] == "Y":
            return y_ref.at[:, pl.ds(pl.multiple_of(y_mine + begin, BLK), width)]
        return x_ref.at[:, pl.ds(pl.multiple_of(x_mine + begin, 128), width)]

    def neighbour(axis, direction):
        step = turn * direction
        return (
            lax.rem(x + step + NX, NX) if axis == "x" else x,
            lax.rem(z + step + NZ, NZ) if axis == "z" else z,
            lax.rem(y + step + NY, NY) if axis == "y" else y,
            c,
        )

    def pass_on(piece):
        for axis, direction, seen in onward(piece):
            pltpu.make_async_remote_copy(
                src_ref=source(piece),
                dst_ref=slot(piece),
                send_sem={"Y": y_send, "C": code_send}.get(piece[0][0], x_send),
                recv_sem=got.at[index[seen]],
                device_id=neighbour(axis, direction * way(piece[0])),
                device_id_type=MESH,
            ).start()

    for piece in first:
        pass_on(piece)

    info = info_all.at[x * NC + c]

    def do_y_squares(begin):
        if begin == 0:
            own.wait()
        for k in range(begin, begin + 8):
            info[1, k : k + 1, :] = squares_of(y_own[:, k * BLK : (k + 1) * BLK])

    def do_info():
        for k in range(HALF):
            g_row = g_ref[pl.ds(pl.multiple_of((c * HALF + k) * BLK, BLK), BLK)]
            info[0, k : k + 1, :] = OFFSET * g_row.astype(jnp.float32).reshape(1, BLK)
        for device in line_peers + [sibling]:
            pltpu.make_async_remote_copy(
                src_ref=info,
                dst_ref=info,
                send_sem=info_sem.at[0],
                recv_sem=info_sem.at[1],
                device_id=device,
                device_id_type=MESH,
            ).start()

    def over_codes():
        return pltpu.make_async_remote_copy(
            src_ref=codes.at[c],
            dst_ref=codes.at[c],
            send_sem=code_sem.at[0],
            recv_sem=code_sem.at[1],
            device_id=sibling,
            device_id_type=MESH,
        )

    table = {}
    steps = 4

    def do_table():
        over_codes().wait()
        halves = [codes[k].reshape(LINES, WIDE) for k in range(NC)]
        lane = lax.broadcasted_iota(jnp.int32, (LINES, WIDE), 1)
        turned = [pltpu.roll(part, WIDE // 2, 1) for part in halves]
        even = jnp.where(lane < WIDE // 2, halves[0], turned[1])
        odd = jnp.where(lane < WIDE // 2, turned[0], halves[1])
        entry = jnp.where(c == 0, even, odd)
        owner = entry // HALF
        match = (entry >= 0) & (owner % LINES == line)
        row = (
            lax.broadcasted_iota(jnp.int32, entry.shape, 0) * HALF_RB
            + lane % (WIDE // 2) // KH
        )
        col = owner // LINES * TB_DEV + lane // (WIDE // 2) * HALF + entry % HALF
        hits = match.astype(jnp.float32)
        down, over = (lax.broadcasted_iota(jnp.int32, (WIDE, WIDE), k) for k in range(2))
        left = exact(hits, (down < over).astype(jnp.float32))
        totals = exact(hits, jnp.ones((WIDE, WIDE), jnp.float32))
        down, over = (lax.broadcasted_iota(jnp.int32, (LINES, LINES), k) for k in range(2))
        above = exact((over < down).astype(jnp.float32), totals)
        table["code"] = (row * STRIDE + col).astype(jnp.float32)
        table["spot"] = jnp.where(match, left + above, -1.0)
        table["count"] = jnp.sum(totals, axis=0, keepdims=True)
        table["found"] = jnp.zeros((MOST, WIDE), jnp.float32)

    def do_find(begin):
        spots = lax.broadcasted_iota(jnp.int32, (MOST, WIDE), 0).astype(jnp.float32)
        for k in range(begin, begin + LINES // steps):
            row = slice(k, k + 1)
            table["found"] += jnp.where(table["spot"][row] == spots, table["code"][row], 0.0)

    def do_items():
        items = lax.dot_general(
            jnp.ones((8, WIDE), jnp.float32),
            table["found"],
            (((1,), (1,)), ((), ())),
            preferred_element_type=jnp.float32,
            precision=lax.Precision.HIGHEST,
        )
        many = jnp.concatenate([table["count"]] * (MOST // WIDE), axis=1)
        spot = lax.broadcasted_iota(jnp.int32, (8, MOST), 1).astype(jnp.float32)
        items = jnp.where(spot < many, items, float(NONE))
        at = lax.broadcasted_iota(jnp.int32, (8, MOST), 0)
        items_ref[...] = jnp.where(at == 0, items, many).astype(jnp.int32)

    early = [functools.partial(do_y_squares, k) for k in range(0, HALF, 8)]
    early += [do_info]
    late = [do_table]
    late += [functools.partial(do_find, k) for k in range(0, LINES, LINES // steps)]
    late += [do_items]
    codes_left, between = LINES - 1, 0
    for piece in order:
        here = slot(piece)
        pltpu.make_async_copy(here, here, got.at[index[piece]]).wait()
        pass_on(piece)
        if piece[0] == "C":
            codes_left -= 1
            if codes_left == 0:
                over_codes().start()
            continue
        if piece[0][0] == "Y":
            pltpu.make_async_remote_copy(
                src_ref=here,
                dst_ref=here,
                send_sem=pair_sem.at[0],
                recv_sem=pair_sem.at[1],
                device_id=sibling,
                device_id_type=MESH,
            ).start()
        between += 1
        if between % 3 == 0:
            if early:
                early.pop(0)()
            elif late and codes_left == 0:
                late.pop(0)()
    for task in early + late:
        task()

    for copy in keeps:
        copy.wait()
    most = x_all.at[pl.ds(0, LINES - 1)]
    pltpu.make_async_copy(most, most, x_send).wait()
    most = y_all.at[pl.ds(0, NX - 1), :, pl.ds(0, Y_LANES)]
    for semaphore in (y_send, pair_sem.at[0], pair_sem.at[1]):
        pltpu.make_async_copy(most, most, semaphore).wait()
    most = info_all.at[pl.ds(0, NX * NC - 1)]
    for side in range(2):
        pltpu.make_async_copy(most, most, info_sem.at[side]).wait()
    most = codes.at[0, pl.ds(0, LINES - 1)]
    pltpu.make_async_copy(most, most, code_send).wait()


def gather(x_src, y_tgt, g_rows, owners, locals_, lives):
    count = len(gather_plan()[1])
    dma = pltpu.SemaphoreType.DMA
    hbm = pl.BlockSpec(memory_space=pltpu.HBM)
    return pl.pallas_call(
        gather_kernel,
        out_shape=(
            pltpu.VMEM((LINES, DIM, X_LANES), jnp.bfloat16),
            pltpu.VMEM((NX, DIM, NC * Y_LANES), jnp.bfloat16),
            jax.ShapeDtypeStruct((NX * NC, 2, HALF, BLK), jnp.float32),
            jax.ShapeDtypeStruct((8, MOST), jnp.int32),
        ),
        in_specs=[hbm] * 6,
        out_specs=(VMEM, VMEM, VMEM, VMEM),
        scratch_shapes=[
            pltpu.VMEM((NC, LINES, 1, WIDE), jnp.int32),
            pltpu.VMEM((DIM, Y_LANES), jnp.bfloat16),
            pltpu.VMEM(g_rows.shape, jnp.bfloat16),
            pltpu.VMEM(owners.shape, jnp.int32),
            pltpu.VMEM(locals_.shape, jnp.int32),
            pltpu.VMEM(lives.shape, jnp.int32),
            dma((4,)),
            dma((2,)),
            dma((2,)),
            dma,
            dma,
            dma((2,)),
            dma,
            dma,
            dma((2,)),
            dma((count,)),
        ],
        compiler_params=pltpu.CompilerParams(
            collective_id=0, has_side_effects=True, vmem_limit_bytes=26 * 1024 * 1024
        ),
        name="gather",
    )(x_src, y_tgt, g_rows, owners, locals_, lives)


def potential(logit2):
    logit = logit2 * LN2
    top = jnp.maximum(logit, 0.0)
    return -EPSILON * (top + jnp.log(jnp.exp(-top) + jnp.exp(logit - top)))


def merged(parts):
    top = functools.reduce(jnp.maximum, parts)
    return top + jnp.log2(sum(jnp.exp2(part - top) for part in parts))


def exchange_kernel(
    part_ref, w_ref, f_ref, bias_ref, parts, part_sem, bias_sem, f_sem
):
    x, z, y, c = place()
    group = LINES
    me = z * NY + y

    def apart(size, step):
        return min(step, size - step)

    steps = [(dz, dy) for dz in range(NZ) for dy in range(NY) if dz or dy]
    steps.sort(key=lambda by: -apart(NZ, by[0]) * NY - apart(NY, by[1]))
    zs, ys = ([lax.rem(at + k, size) for k in range(size)] for at, size in ((z, NZ), (y, NY)))
    peers = [(zs[dz] * NY + ys[dy], (x, zs[dz], ys[dy], c)) for dz, dy in steps]

    barrier = pltpu.get_barrier_semaphore()

    sibling = (x, z, y, 1 - c)
    pl.semaphore_signal(barrier, inc=1, device_id=sibling, device_id_type=MESH)
    for _, device in peers:
        pl.semaphore_signal(barrier, inc=1, device_id=device, device_id_type=MESH)
    pl.semaphore_wait(barrier, group)
    for other, device in peers:
        pltpu.make_async_remote_copy(
            src_ref=part_ref.at[other],
            dst_ref=parts.at[me],
            send_sem=part_sem.at[0],
            recv_sem=part_sem.at[1],
            device_id=device,
            device_id_type=MESH,
        ).start()
    parts[me] = part_ref[me]
    others = parts.at[pl.ds(0, group - 1)]
    pltpu.make_async_copy(others, others, part_sem.at[1]).wait()
    f_half = potential(merged([parts[k] for k in range(group)]))
    for k in range(HALF_RB):
        f_ref[pl.ds(pl.multiple_of((c * HALF_RB + k) * BLK, BLK), BLK)] = f_half[k]
    mine = pl.ds(pl.multiple_of(c * X_LANES, X_LANES), X_LANES)
    w_half = [
        w_ref[pl.ds(pl.multiple_of((c * HALF_RB + k) * BLK, BLK), BLK)].reshape(1, BLK)
        for k in range(HALF_RB)
    ]
    bias_ref[me] = OFFSET * f_half + (EPSILON * OFFSET) * jnp.concatenate(w_half, axis=0)

    for _, device in peers:
        pltpu.make_async_remote_copy(
            src_ref=bias_ref.at[me],
            dst_ref=bias_ref.at[me],
            send_sem=bias_sem.at[0],
            recv_sem=bias_sem.at[1],
            device_id=device,
            device_id_type=MESH,
        ).start()
    over = pltpu.make_async_remote_copy(
        src_ref=f_ref.at[mine],
        dst_ref=f_ref.at[mine],
        send_sem=f_sem.at[0],
        recv_sem=f_sem.at[1],
        device_id=sibling,
        device_id_type=MESH,
    )
    over.start()
    pltpu.make_async_copy(others, others, part_sem.at[0]).wait()
    others = bias_ref.at[pl.ds(0, group - 1)]
    for side in range(2):
        pltpu.make_async_copy(others, others, bias_sem.at[side]).wait()
    over.wait()


def exchange(partial, w_rows):
    dma = pltpu.SemaphoreType.DMA
    group = LINES
    return pl.pallas_call(
        exchange_kernel,
        out_shape=(
            jax.ShapeDtypeStruct((RB_DEV * BLK,), jnp.float32),
            jax.ShapeDtypeStruct((group, HALF_RB, BLK), jnp.float32),
        ),
        in_specs=[VMEM, VMEM],
        out_specs=(VMEM, VMEM),
        scratch_shapes=[
            pltpu.VMEM((group, HALF_RB, BLK), jnp.float32),
            dma((2,)),
            dma((2,)),
            dma((2,)),
        ],
        compiler_params=pltpu.CompilerParams(
            collective_id=1, has_side_effects=True, vmem_limit_bytes=16 * 1024 * 1024
        ),
        name="exchange",
    )(partial, w_rows)


def finish_kernel(part_ref, g_ref, parts, part_sem, g_sem):
    x, z, y, c = place()
    barrier = pltpu.get_barrier_semaphore()
    group = NX * NC
    me = x * NC + c
    peers = [lax.rem(me + k, group) for k in range(1, group)]
    sibling = (x, z, y, 1 - c)
    for other in peers:
        pl.semaphore_signal(
            barrier, inc=1, device_id=(other // NC, z, y, other % NC), device_id_type=MESH
        )
    pl.semaphore_wait(barrier, group - 1)
    for other in peers:
        pltpu.make_async_remote_copy(
            src_ref=part_ref.at[other],
            dst_ref=parts.at[me],
            send_sem=part_sem.at[0],
            recv_sem=part_sem.at[1],
            device_id=(other // NC, z, y, other % NC),
            device_id_type=MESH,
        ).start()
    parts[me] = part_ref[me]
    others = parts.at[pl.ds(0, group - 1)]
    pltpu.make_async_copy(others, others, part_sem.at[1]).wait()
    g_half = potential(merged([parts[k] for k in range(group)]))
    for k in range(HALF):
        g_ref[pl.ds(pl.multiple_of((c * HALF + k) * BLK, BLK), BLK)] = g_half[k]
    mine = pl.ds(pl.multiple_of(c * Y_LANES, Y_LANES), Y_LANES)
    over = pltpu.make_async_remote_copy(
        src_ref=g_ref.at[mine],
        dst_ref=g_ref.at[mine],
        send_sem=g_sem.at[0],
        recv_sem=g_sem.at[1],
        device_id=sibling,
        device_id_type=MESH,
    )
    over.start()
    pltpu.make_async_copy(others, others, part_sem.at[0]).wait()
    over.wait()


def finish(partial):
    dma = pltpu.SemaphoreType.DMA
    return pl.pallas_call(
        finish_kernel,
        out_shape=jax.ShapeDtypeStruct((TB_DEV * BLK,), jnp.float32),
        in_specs=[VMEM],
        out_specs=VMEM,
        scratch_shapes=[pltpu.VMEM((NX * NC, HALF, BLK), jnp.float32), dma((2,)), dma((2,))],
        compiler_params=pltpu.CompilerParams(
            collective_id=2, has_side_effects=True, vmem_limit_bytes=16 * 1024 * 1024
        ),
        name="finish",
    )(partial)


def on_device(x_src, w_src, y_tgt, g_in, support_owner, support_local, live_count):
    f32 = jnp.float32
    small = (
        g_in,
        jnp.swapaxes(support_owner, 1, 2),
        jnp.swapaxes(support_local, 1, 2),
        live_count,
    )
    given = [
        pltpu.with_memory_space_constraint(array, pltpu.HBM) for array in (x_src, y_tgt, *small)
    ]
    x_all, y_all, info, items = gather(*given)
    shared = (items, x_all, y_all, info)
    scratch = [pltpu.VMEM((NX * NC + 1, ROWS, BLK), f32), pltpu.VMEM((NX * NC, HALF, BLK), f32)]
    partial = local_call(row_kernel, 3, ROWS, scratch, "rows")(*shared)
    f_new, offsets = exchange(
        partial.reshape(LINES, HALF_RB, BLK), w_src
    )
    scratch = [pltpu.VMEM((NONE + 8, BLK), f32)] * 2
    col = local_call(column_kernel, 4, NONE, scratch, "columns")(
        *shared, offsets.reshape(ROWS, BLK)
    )
    g_new = finish(col.reshape(NX * NC, HALF, BLK))
    return f_new, g_new


def solution(mesh):
    fine = Mesh(mesh.devices.reshape(NX, NZ, NY, NC), ("x", "z", "y", "core"))
    src = ("x", "z", "y")
    placed = (
        P(None, src),
        P(src),
        P(None, src),
        P(src),
        P("core", src, None),
        P("core", src, None),
        P("core", src),
    )
    return jax.shard_map(
        on_device, mesh=fine, in_specs=placed, out_specs=(P(src), P(src)), check_vma=False
    )
```

```python
import functools
import heapq

import jax
import jax.numpy as jnp
import numpy as np
from jax import lax
from jax.experimental import pallas as pl
from jax.experimental.pallas import tpu as pltpu
from jax.sharding import Mesh, PartitionSpec as P

DIM = 64
BLK = 256
KH = 8
RB_DEV = 16
TB_DEV = 64
HALF = TB_DEV // 2

EPSILON = 0.1
EMPTY = -1e30
PER = 2.0 / (DIM * EPSILON)
PER2 = PER * float(np.log2(np.e))
OFFSET = DIM / 2.0
LN2 = float(np.log(2.0))
AUG = 16

MESH = pl.DeviceIdType.MESH
NX, NZ, NY, NC = 4, 8, 4, 2
LINES = NZ * NY
HALF_RB = RB_DEV // 2
ROWS = LINES * HALF_RB
NONE = NX * TB_DEV
STRIDE = 2 * NONE
MOST = LINES * 2 * NX * NC
WIDE = RB_DEV * KH
X_LANES = HALF_RB * BLK
Y_LANES = HALF * BLK
UNROLL = 32
REST = 8
SAFE = 100.0


def extra_rows(row, at_left):
    high = row.astype(jnp.bfloat16).astype(jnp.float32)
    middle = (row - high).astype(jnp.bfloat16).astype(jnp.float32)
    low = row - high - middle
    at = lax.broadcasted_iota(jnp.int32, (AUG, BLK), 0)
    base = 0 if at_left else 3
    ones = jnp.where(at < 6, 1.0, 0.0)
    parts = jnp.where(at == base + 1, middle, jnp.where(at == base + 2, low, ones))
    return jnp.where(at == base, high, parts).astype(jnp.bfloat16)


def squares_of(tile):
    return 0.5 * jnp.sum(jnp.square(tile.astype(jnp.float32)), axis=0, keepdims=True)


def log2_mass(mass):
    return jnp.maximum(jnp.log2(mass), EMPTY)


def tile_logits(left, right):
    return lax.dot_general(
        left, right, (((0,), (0,)), ((), ())), preferred_element_type=jnp.float32
    )


def peak_and_mass(tile):
    peak = jnp.max(tile, axis=0, keepdims=True)
    mass = jnp.sum(jnp.exp2((tile - peak) * PER2), axis=0, keepdims=True)
    return peak, mass


def lane_block(index):
    return pl.ds(pl.multiple_of(index * BLK, BLK), BLK)


def x_tile(x_ref, block):
    return x_ref[block // HALF_RB, :, lane_block(block % HALF_RB)]


def y_tile(y_ref, block):
    return y_ref[block // TB_DEV, :, lane_block(block % TB_DEV)]


def for_pairs(items_ref, visit):
    def groups(size, first, last):
        def step(group, carry):
            for k in range(size):
                code = items_ref[0, first + group * size + k]
                visit(code // STRIDE, code % STRIDE)
            return carry

        lax.fori_loop(0, (last - first + size - 1) // size, step, 0)

    count = items_ref[1, 0]
    whole = count // UNROLL * UNROLL
    groups(UNROLL, 0, whole)
    groups(REST, whole, count)


def plain_mass(tile):
    return jnp.sum(jnp.exp2(tile * PER2), axis=0, keepdims=True)


def one_of(col):
    return col // HALF, pl.ds(col % HALF, 1)


def row_kernel(items_ref, x_ref, y_ref, info_ref, out_ref, slots, bias):
    bias[...] = info_ref[:, 0] - info_ref[:, 1]
    safe = jnp.max(info_ref[:, 0]) * PER2 <= SAFE

    def logits(row, col):
        half, at = one_of(col % NONE)
        left = jnp.concatenate(
            [y_tile(y_ref, col % NONE), extra_rows(bias[half, at, :], True)], axis=0
        )
        tile = x_tile(x_ref, row)
        right = jnp.concatenate([tile, extra_rows(-squares_of(tile), False)], axis=0)
        return tile_logits(left, right)

    @pl.when(safe)
    def _():
        slots[...] = jnp.zeros(slots.shape, jnp.float32)

        def visit(row, col):
            slots[col // HALF, pl.ds(row, 1), :] = plain_mass(logits(row, col))

        for_pairs(items_ref, visit)
        out_ref[...] = log2_mass(sum(slots[k] for k in range(NC * NX)))

    @pl.when(jnp.logical_not(safe))
    def _():
        slots[...] = jnp.full(slots.shape, EMPTY, jnp.float32)

        def visit(row, col):
            peak, mass = peak_and_mass(logits(row, col))
            slots[col // HALF, pl.ds(row, 1), :] = peak * PER2 + jnp.log2(mass)

        for_pairs(items_ref, visit)
        out_ref[...] = merged([slots[k] for k in range(NC * NX)])


def column_kernel(
    items_ref, x_ref, y_ref, info_ref, offset_ref, out_ref, peaks, masses
):
    masses[...] = jnp.zeros(masses.shape, jnp.float32)
    safe = jnp.max(offset_ref[...]) * PER2 <= SAFE

    def logits(row, col):
        half, at = one_of(col % NONE)
        tile = x_tile(x_ref, row)
        bias = offset_ref[pl.ds(row, 1), :] - squares_of(tile)
        left = jnp.concatenate([tile, extra_rows(bias, True)], axis=0)
        square = info_ref[half, 1, at, :]
        right = jnp.concatenate(
            [y_tile(y_ref, col % NONE), extra_rows(-square, False)], axis=0
        )
        return tile_logits(left, right)

    @pl.when(safe)
    def _():
        def visit(row, col):
            masses[pl.ds(col, 1), :] += plain_mass(logits(row, col))

        for_pairs(items_ref, visit)
        out_ref[...] = log2_mass(masses[0:NONE, :])

    @pl.when(jnp.logical_not(safe))
    def _():
        peaks[...] = jnp.full(peaks.shape, EMPTY, jnp.float32)

        def visit(row, col):
            peak, mass = peak_and_mass(logits(row, col))
            old = peaks[pl.ds(col, 1), :]
            new = jnp.maximum(old, peak)
            peaks[pl.ds(col, 1), :] = new
            masses[pl.ds(col, 1), :] = masses[pl.ds(col, 1), :] * jnp.exp2(
                (old - new) * PER2
            ) + mass * jnp.exp2((peak - new) * PER2)

        for_pairs(items_ref, visit)
        out_ref[...] = jnp.maximum(
            peaks[0:NONE, :] * PER2 + log2_mass(masses[0:NONE, :]), EMPTY
        )


SMEM = pl.BlockSpec(memory_space=pltpu.SMEM)
VMEM = pl.BlockSpec(memory_space=pltpu.VMEM)


def local_call(body, arrays, out_rows, scratch, name):
    return pl.pallas_call(
        body,
        out_shape=jax.ShapeDtypeStruct((out_rows, BLK), jnp.float32),
        in_specs=[SMEM] + [VMEM] * arrays,
        out_specs=VMEM,
        scratch_shapes=scratch,
        compiler_params=pltpu.CompilerParams(vmem_limit_bytes=26 * 1024 * 1024),
        name=name,
    )


FIRST = ("Bl", "Bh", "A")
PARTS = {"A": (0, 768, 1), "Bl": (768, 512, -1), "Bh": (1280, 768, 1)}
Y_CHUNKS = 4
CHUNK = Y_LANES // Y_CHUNKS


def place():
    return tuple(lax.axis_index(axis) for axis in ("x", "z", "y", "core"))


def moved(size, offset):
    longest = {8: 4, 4: 2}[size]
    shortest = size - 1 - longest
    out = []
    if -longest < offset <= 0:
        out.append((1, offset - 1))
    if 0 <= offset < shortest:
        out.append((-1, offset + 1))
    return out


def way(kind):
    if kind in PARTS:
        return PARTS[kind][2]
    return -1 if kind[0] == "Y" and int(kind[1:]) % 2 else 1


def onward(piece):
    kind, a, b = piece
    if kind[0] == "A":
        found = [("z", d, (kind, n, b)) for d, n in moved(NZ, a)]
        if a == 0:
            found += [("y", d, (kind, 0, n)) for d, n in moved(NY, b)]
    elif kind[0] in "BC":
        found = [("z", d, (kind, n, 0)) for d, n in moved(NZ, a)] if b == 0 else []
        found += [("y", d, (kind, a, n)) for d, n in moved(NY, b)]
    else:
        found = [("x", d, (kind, n, 0)) for d, n in moved(NX, a)]
    return found


def gather_plan():
    took = {kind: part[1] for kind, part in PARTS.items()} | {"C": 4}
    kinds = [f"Y{k}" for k in range(Y_CHUNKS)]
    took |= {kind: CHUNK for kind in kinds}
    first = [(kind, 0, 0) for kind in ["C", *FIRST, *kinds]]
    free, waiting, order = {}, [], []

    def send(now, piece):
        for axis, direction, seen in onward(piece):
            link = (axis, direction * way(piece[0]))
            end = max(now, free.get(link, 0.0)) + took[piece[0]]
            free[link] = end
            heapq.heappush(waiting, (end + 384.0, seen))

    for piece in first:
        send(0.0, piece)
    while waiting:
        now, piece = heapq.heappop(waiting)
        order.append(piece)
        send(now, piece)
    return first, order


def gather_kernel(
    x_ref, y_ref, g_hbm, owner_hbm, local_hbm, live_hbm,
    x_all, y_all, info_all, items_ref,
    codes, y_own, g_ref, owner_ref, local_ref, live_ref, small_sem, info_sem, code_sem, code_send, own_sem, keep_sem, x_send, y_send, pair_sem, got,
):
    x, z, y, c = place()
    turn = 1 - 2 * c
    line = z * NY + y
    first, order = gather_plan()
    index = {piece: k for k, piece in enumerate(order)}

    small = [
        pltpu.make_async_copy(there, here, small_sem.at[k])
        for k, (there, here) in enumerate(
            [(owner_hbm, owner_ref), (local_hbm, local_ref), (live_hbm, live_ref), (g_hbm, g_ref)]
        )
    ]
    for copy in small:
        copy.start()
    barrier = pltpu.get_barrier_semaphore()
    sibling = (x, z, y, 1 - c)

    line_peers = [(lax.rem(x + k, NX), z, y, core) for k in range(1, NX) for core in range(NC)]
    near = [(x, lax.rem(z + k, NZ), y, c) for k in (1, NZ - 1)]
    near += [(x, z, lax.rem(y + k, NY), c) for k in (1, NY - 1)]
    near += [sibling] + line_peers
    for device in near:
        pl.semaphore_signal(barrier, inc=1, device_id=device, device_id_type=MESH)

    x_mine = pl.multiple_of(c * X_LANES, X_LANES)
    y_mine = pl.multiple_of(c * Y_LANES, Y_LANES)
    own = pltpu.make_async_copy(y_ref.at[:, pl.ds(y_mine, Y_LANES)], y_own, own_sem)
    keeps = [
        pltpu.make_async_copy(
            x_ref.at[:, pl.ds(x_mine, X_LANES)], x_all.at[line], keep_sem.at[0]
        ),
        pltpu.make_async_copy(y_ref, y_all.at[x], keep_sem.at[1]),
    ]
    for copy in [own] + keeps:
        copy.start()

    exact = functools.partial(
        jnp.dot, preferred_element_type=jnp.float32, precision=lax.Precision.HIGHEST
    )
    for copy in small:
        copy.wait()
    slot_at = lax.broadcasted_iota(jnp.int32, (KH, RB_DEV), 0)
    listed = owner_ref[0] * HALF + local_ref[0]
    listed = jnp.where(slot_at < live_ref[...], listed, -1).astype(jnp.float32)
    down, over = (lax.broadcasted_iota(jnp.int32, (RB_DEV, WIDE), k) for k in range(2))
    spread = exact(listed, (over // KH == down).astype(jnp.float32))
    down, over = (lax.broadcasted_iota(jnp.int32, (KH, WIDE), k) for k in range(2))
    codes[c, line] = jnp.sum(
        jnp.where(over % KH == down, spread, 0.0), axis=0, keepdims=True
    ).astype(jnp.int32)
    pl.semaphore_wait(barrier, len(near))

    def lanes_of(kind):
        if kind in PARTS:
            return PARTS[kind][:2]
        return int(kind[1:]) * CHUNK, CHUNK

    def slot(piece):
        kind, a, b = piece
        ahead = turn * way(kind)
        origin = lax.rem(z + ahead * a + NZ, NZ) * NY + lax.rem(y + ahead * b + NY, NY)
        if kind == "C":
            return codes.at[c, origin]
        begin, width = lanes_of(kind)
        if kind[0] == "Y":
            there = pl.ds(pl.multiple_of(y_mine + begin, BLK), width)
            return y_all.at[lax.rem(x + ahead * a + NX, NX), :, there]
        return x_all.at[origin, :, pl.ds(begin, width)]

    def source(piece):
        kind, a, b = piece
        if a or b or kind == "C":
            return slot(piece)
        begin, width = lanes_of(kind)
        if kind[0] == "Y":
            return y_ref.at[:, pl.ds(pl.multiple_of(y_mine + begin, BLK), width)]
        return x_ref.at[:, pl.ds(pl.multiple_of(x_mine + begin, 128), width)]

    def neighbour(axis, direction):
        step = turn * direction
        return (
            lax.rem(x + step + NX, NX) if axis == "x" else x,
            lax.rem(z + step + NZ, NZ) if axis == "z" else z,
            lax.rem(y + step + NY, NY) if axis == "y" else y,
            c,
        )

    def pass_on(piece):
        for axis, direction, seen in onward(piece):
            pltpu.make_async_remote_copy(
                src_ref=source(piece),
                dst_ref=slot(piece),
                send_sem={"Y": y_send, "C": code_send}.get(piece[0][0], x_send),
                recv_sem=got.at[index[seen]],
                device_id=neighbour(axis, direction * way(piece[0])),
                device_id_type=MESH,
            ).start()

    for piece in first:
        pass_on(piece)

    info = info_all.at[x * NC + c]

    def do_y_squares(begin):
        if begin == 0:
            own.wait()
        for k in range(begin, begin + 8):
            info[1, k : k + 1, :] = squares_of(y_own[:, k * BLK : (k + 1) * BLK])

    def do_info():
        for k in range(HALF):
            g_row = g_ref[pl.ds(pl.multiple_of((c * HALF + k) * BLK, BLK), BLK)]
            info[0, k : k + 1, :] = OFFSET * g_row.astype(jnp.float32).reshape(1, BLK)
        for device in line_peers + [sibling]:
            pltpu.make_async_remote_copy(
                src_ref=info,
                dst_ref=info,
                send_sem=info_sem.at[0],
                recv_sem=info_sem.at[1],
                device_id=device,
                device_id_type=MESH,
            ).start()

    def over_codes():
        return pltpu.make_async_remote_copy(
            src_ref=codes.at[c],
            dst_ref=codes.at[c],
            send_sem=code_sem.at[0],
            recv_sem=code_sem.at[1],
            device_id=sibling,
            device_id_type=MESH,
        )

    table = {}
    steps = 4

    def do_table():
        over_codes().wait()
        halves = [codes[k].reshape(LINES, WIDE) for k in range(NC)]
        lane = lax.broadcasted_iota(jnp.int32, (LINES, WIDE), 1)
        turned = [pltpu.roll(part, WIDE // 2, 1) for part in halves]
        even = jnp.where(lane < WIDE // 2, halves[0], turned[1])
        odd = jnp.where(lane < WIDE // 2, turned[0], halves[1])
        entry = jnp.where(c == 0, even, odd)
        owner = entry // HALF
        match = (entry >= 0) & (owner % LINES == line)
        row = (
            lax.broadcasted_iota(jnp.int32, entry.shape, 0) * HALF_RB
            + lane % (WIDE // 2) // KH
        )
        col = owner // LINES * TB_DEV + lane // (WIDE // 2) * HALF + entry % HALF
        hits = match.astype(jnp.float32)
        down, over = (lax.broadcasted_iota(jnp.int32, (WIDE, WIDE), k) for k in range(2))
        left = exact(hits, (down < over).astype(jnp.float32))
        totals = exact(hits, jnp.ones((WIDE, WIDE), jnp.float32))
        down, over = (lax.broadcasted_iota(jnp.int32, (LINES, LINES), k) for k in range(2))
        above = exact((over < down).astype(jnp.float32), totals)
        table["code"] = (row * STRIDE + col).astype(jnp.float32)
        table["spot"] = jnp.where(match, left + above, -1.0)
        table["count"] = jnp.sum(totals, axis=0, keepdims=True)
        table["found"] = jnp.zeros((MOST, WIDE), jnp.float32)

    def do_find(begin):
        spots = lax.broadcasted_iota(jnp.int32, (MOST, WIDE), 0).astype(jnp.float32)
        for k in range(begin, begin + LINES // steps):
            row = slice(k, k + 1)
            table["found"] += jnp.where(table["spot"][row] == spots, table["code"][row], 0.0)

    def do_items():
        items = lax.dot_general(
            jnp.ones((8, WIDE), jnp.float32),
            table["found"],
            (((1,), (1,)), ((), ())),
            preferred_element_type=jnp.float32,
            precision=lax.Precision.HIGHEST,
        )
        many = jnp.concatenate([table["count"]] * (MOST // WIDE), axis=1)
        spot = lax.broadcasted_iota(jnp.int32, (8, MOST), 1).astype(jnp.float32)
        items = jnp.where(spot < many, items, float(NONE))
        at = lax.broadcasted_iota(jnp.int32, (8, MOST), 0)
        items_ref[...] = jnp.where(at == 0, items, many).astype(jnp.int32)

    early = [functools.partial(do_y_squares, k) for k in range(0, HALF, 8)]
    early += [do_info]
    late = [do_table]
    late += [functools.partial(do_find, k) for k in range(0, LINES, LINES // steps)]
    late += [do_items]
    codes_left, between = LINES - 1, 0
    for piece in order:
        here = slot(piece)
        pltpu.make_async_copy(here, here, got.at[index[piece]]).wait()
        pass_on(piece)
        if piece[0] == "C":
            codes_left -= 1
            if codes_left == 0:
                over_codes().start()
            continue
        if piece[0][0] == "Y":
            pltpu.make_async_remote_copy(
                src_ref=here,
                dst_ref=here,
                send_sem=pair_sem.at[0],
                recv_sem=pair_sem.at[1],
                device_id=sibling,
                device_id_type=MESH,
            ).start()
        between += 1
        if between % 3 == 0:
            if early:
                early.pop(0)()
            elif late and codes_left == 0:
                late.pop(0)()
    for task in early + late:
        task()

    for copy in keeps:
        copy.wait()
    most = x_all.at[pl.ds(0, LINES - 1)]
    pltpu.make_async_copy(most, most, x_send).wait()
    most = y_all.at[pl.ds(0, NX - 1), :, pl.ds(0, Y_LANES)]
    for semaphore in (y_send, pair_sem.at[0], pair_sem.at[1]):
        pltpu.make_async_copy(most, most, semaphore).wait()
    most = info_all.at[pl.ds(0, NX * NC - 1)]
    for side in range(2):
        pltpu.make_async_copy(most, most, info_sem.at[side]).wait()
    most = codes.at[0, pl.ds(0, LINES - 1)]
    pltpu.make_async_copy(most, most, code_send).wait()


def gather(x_src, y_tgt, g_rows, owners, locals_, lives):
    count = len(gather_plan()[1])
    dma = pltpu.SemaphoreType.DMA
    hbm = pl.BlockSpec(memory_space=pltpu.HBM)
    return pl.pallas_call(
        gather_kernel,
        out_shape=(
            pltpu.VMEM((LINES, DIM, X_LANES), jnp.bfloat16),
            pltpu.VMEM((NX, DIM, NC * Y_LANES), jnp.bfloat16),
            jax.ShapeDtypeStruct((NX * NC, 2, HALF, BLK), jnp.float32),
            jax.ShapeDtypeStruct((8, MOST), jnp.int32),
        ),
        in_specs=[hbm] * 6,
        out_specs=(VMEM, VMEM, VMEM, VMEM),
        scratch_shapes=[
            pltpu.VMEM((NC, LINES, 1, WIDE), jnp.int32),
            pltpu.VMEM((DIM, Y_LANES), jnp.bfloat16),
            pltpu.VMEM(g_rows.shape, jnp.bfloat16),
            pltpu.VMEM(owners.shape, jnp.int32),
            pltpu.VMEM(locals_.shape, jnp.int32),
            pltpu.VMEM(lives.shape, jnp.int32),
            dma((4,)),
            dma((2,)),
            dma((2,)),
            dma,
            dma,
            dma((2,)),
            dma,
            dma,
            dma((2,)),
            dma((count,)),
        ],
        compiler_params=pltpu.CompilerParams(
            collective_id=0, has_side_effects=True, vmem_limit_bytes=26 * 1024 * 1024
        ),
        name="gather",
    )(x_src, y_tgt, g_rows, owners, locals_, lives)


def potential(logit2):
    logit = logit2 * LN2
    top = jnp.maximum(logit, 0.0)
    return -EPSILON * (top + jnp.log(jnp.exp(-top) + jnp.exp(logit - top)))


def merged(parts):
    top = functools.reduce(jnp.maximum, parts)
    return top + jnp.log2(sum(jnp.exp2(part - top) for part in parts))


def exchange_kernel(
    part_ref, w_ref, f_ref, bias_ref, parts, part_sem, bias_sem, f_sem
):
    x, z, y, c = place()
    group = LINES
    me = z * NY + y

    def apart(size, step):
        return min(step, size - step)

    steps = [(dz, dy) for dz in range(NZ) for dy in range(NY) if dz or dy]
    steps.sort(key=lambda by: -apart(NZ, by[0]) * NY - apart(NY, by[1]))
    zs, ys = ([lax.rem(at + k, size) for k in range(size)] for at, size in ((z, NZ), (y, NY)))
    peers = [(zs[dz] * NY + ys[dy], (x, zs[dz], ys[dy], c)) for dz, dy in steps]

    barrier = pltpu.get_barrier_semaphore()

    sibling = (x, z, y, 1 - c)
    pl.semaphore_signal(barrier, inc=1, device_id=sibling, device_id_type=MESH)
    for _, device in peers:
        pl.semaphore_signal(barrier, inc=1, device_id=device, device_id_type=MESH)
    pl.semaphore_wait(barrier, group)
    for other, device in peers:
        pltpu.make_async_remote_copy(
            src_ref=part_ref.at[other],
            dst_ref=parts.at[me],
            send_sem=part_sem.at[0],
            recv_sem=part_sem.at[1],
            device_id=device,
            device_id_type=MESH,
        ).start()
    parts[me] = part_ref[me]
    others = parts.at[pl.ds(0, group - 1)]
    pltpu.make_async_copy(others, others, part_sem.at[1]).wait()
    f_half = potential(merged([parts[k] for k in range(group)]))
    for k in range(HALF_RB):
        f_ref[pl.ds(pl.multiple_of((c * HALF_RB + k) * BLK, BLK), BLK)] = f_half[k]
    mine = pl.ds(pl.multiple_of(c * X_LANES, X_LANES), X_LANES)
    w_half = [
        w_ref[pl.ds(pl.multiple_of((c * HALF_RB + k) * BLK, BLK), BLK)].reshape(1, BLK)
        for k in range(HALF_RB)
    ]
    bias_ref[me] = OFFSET * f_half + (EPSILON * OFFSET) * jnp.concatenate(w_half, axis=0)

    for _, device in peers:
        pltpu.make_async_remote_copy(
            src_ref=bias_ref.at[me],
            dst_ref=bias_ref.at[me],
            send_sem=bias_sem.at[0],
            recv_sem=bias_sem.at[1],
            device_id=device,
            device_id_type=MESH,
        ).start()
    over = pltpu.make_async_remote_copy(
        src_ref=f_ref.at[mine],
        dst_ref=f_ref.at[mine],
        send_sem=f_sem.at[0],
        recv_sem=f_sem.at[1],
        device_id=sibling,
        device_id_type=MESH,
    )
    over.start()
    pltpu.make_async_copy(others, others, part_sem.at[0]).wait()
    others = bias_ref.at[pl.ds(0, group - 1)]
    for side in range(2):
        pltpu.make_async_copy(others, others, bias_sem.at[side]).wait()
    over.wait()


def exchange(partial, w_rows):
    dma = pltpu.SemaphoreType.DMA
    group = LINES
    return pl.pallas_call(
        exchange_kernel,
        out_shape=(
            jax.ShapeDtypeStruct((RB_DEV * BLK,), jnp.float32),
            jax.ShapeDtypeStruct((group, HALF_RB, BLK), jnp.float32),
        ),
        in_specs=[VMEM, VMEM],
        out_specs=(VMEM, VMEM),
        scratch_shapes=[
            pltpu.VMEM((group, HALF_RB, BLK), jnp.float32),
            dma((2,)),
            dma((2,)),
            dma((2,)),
        ],
        compiler_params=pltpu.CompilerParams(
            collective_id=1, has_side_effects=True, vmem_limit_bytes=16 * 1024 * 1024
        ),
        name="exchange",
    )(partial, w_rows)


def finish_kernel(part_ref, g_ref, parts, part_sem, g_sem):
    x, z, y, c = place()
    barrier = pltpu.get_barrier_semaphore()
    group = NX * NC
    me = x * NC + c
    peers = [lax.rem(me + k, group) for k in range(1, group)]
    sibling = (x, z, y, 1 - c)
    for other in peers:
        pl.semaphore_signal(
            barrier, inc=1, device_id=(other // NC, z, y, other % NC), device_id_type=MESH
        )
    pl.semaphore_wait(barrier, group - 1)
    for other in peers:
        pltpu.make_async_remote_copy(
            src_ref=part_ref.at[other],
            dst_ref=parts.at[me],
            send_sem=part_sem.at[0],
            recv_sem=part_sem.at[1],
            device_id=(other // NC, z, y, other % NC),
            device_id_type=MESH,
        ).start()
    parts[me] = part_ref[me]
    others = parts.at[pl.ds(0, group - 1)]
    pltpu.make_async_copy(others, others, part_sem.at[1]).wait()
    g_half = potential(merged([parts[k] for k in range(group)]))
    for k in range(HALF):
        g_ref[pl.ds(pl.multiple_of((c * HALF + k) * BLK, BLK), BLK)] = g_half[k]
    mine = pl.ds(pl.multiple_of(c * Y_LANES, Y_LANES), Y_LANES)
    over = pltpu.make_async_remote_copy(
        src_ref=g_ref.at[mine],
        dst_ref=g_ref.at[mine],
        send_sem=g_sem.at[0],
        recv_sem=g_sem.at[1],
        device_id=sibling,
        device_id_type=MESH,
    )
    over.start()
    pltpu.make_async_copy(others, others, part_sem.at[0]).wait()
    over.wait()


def finish(partial):
    dma = pltpu.SemaphoreType.DMA
    return pl.pallas_call(
        finish_kernel,
        out_shape=jax.ShapeDtypeStruct((TB_DEV * BLK,), jnp.float32),
        in_specs=[VMEM],
        out_specs=VMEM,
        scratch_shapes=[pltpu.VMEM((NX * NC, HALF, BLK), jnp.float32), dma((2,)), dma((2,))],
        compiler_params=pltpu.CompilerParams(
            collective_id=2, has_side_effects=True, vmem_limit_bytes=16 * 1024 * 1024
        ),
        name="finish",
    )(partial)


def on_device(x_src, w_src, y_tgt, g_in, support_owner, support_local, live_count):
    f32 = jnp.float32
    small = (
        g_in,
        jnp.swapaxes(support_owner, 1, 2),
        jnp.swapaxes(support_local, 1, 2),
        live_count,
    )
    given = [
        pltpu.with_memory_space_constraint(array, pltpu.HBM) for array in (x_src, y_tgt, *small)
    ]
    x_all, y_all, info, items = gather(*given)
    shared = (items, x_all, y_all, info)
    scratch = [pltpu.VMEM((NX * NC + 1, ROWS, BLK), f32), pltpu.VMEM((NX * NC, HALF, BLK), f32)]
    partial = local_call(row_kernel, 3, ROWS, scratch, "rows")(*shared)
    f_new, offsets = exchange(
        partial.reshape(LINES, HALF_RB, BLK), w_src
    )
    scratch = [pltpu.VMEM((NONE + 8, BLK), f32)] * 2
    col = local_call(column_kernel, 4, NONE, scratch, "columns")(
        *shared, offsets.reshape(ROWS, BLK)
    )
    g_new = finish(col.reshape(NX * NC, HALF, BLK))
    return f_new, g_new


def solution(mesh):
    fine = Mesh(mesh.devices.reshape(NX, NZ, NY, NC), ("x", "z", "y", "core"))
    src = ("x", "z", "y")
    placed = (
        P(None, src),
        P(src),
        P(None, src),
        P(src),
        P("core", src, None),
        P("core", src, None),
        P("core", src),
    )
    return jax.shard_map(
        on_device, mesh=fine, in_specs=placed, out_specs=(P(src), P(src)), check_vma=False
    )
```
